128 devices in a mesh: slab: 16 (over y, x), mp: 8 (over z, core), dp: 1.
Axes of the slice: x: 4, y: 4, z: 4, core: 2. Of those that a mesh axis runs over, the one named last changes fastest.
Arguments:
- enc_feat: bfloat16 [64, 512, 256], P(('dp', 'slab'), 'mp'), may hold values from -120 to 120
- gn_gain: float32 [512], P('mp'), may hold values from 0.1 to 1.9
- gn_bias: float32 [512], P('mp'), may hold values from -3 to 3
- conv_w: bfloat16 [512, 432], P('mp'), may hold values from -0.0546875 to 0.0546875
- clip_frames: int32 [4], P('dp'), may hold values from 1 to 32, 64 in all
- clip_res: int32 [4, 2], P('dp'), may hold values from 8 to 16, as said below
- token_place: int32 [4096], P(('dp', 'slab')), may hold values from 0 to 4095, each once
- embed_w: bfloat16 [64, 3072], replicated, may hold values from -0.75 to 0.75
- embed_b: float32 [3072], replicated, may hold values from -3 to 3
- mod_shift: float32 [3072], P('dp'), may hold values from -3 to 3
- mod_scale: float32 [3072], P('dp'), may hold values from -2 to 2
- mod_gate: float32 [3072], P('dp'), may hold values from -4 to 4
- w_qkv: bfloat16 [3072, 6144], P(None, 'mp'), may hold values from -0.109375 to 0.109375
- q_gain: float32 [128], replicated, may hold values from 0.1 to 1.9
- k_gain: float32 [128], replicated, may hold values from 0.1 to 1.9
- w_out: bfloat16 [2048, 3072], P('mp'), may hold values from -0.125 to 0.125
- grad_out: bfloat16 [4096, 3072], P(('dp', 'slab'), 'mp'), may hold values from -6 to 6
Outputs:
- latents: float32 [64, 16, 256], P(('dp', 'slab'))
- block_out: bfloat16 [4096, 3072], P(('dp', 'slab'), 'mp')
- g_qkv: float32 [3072, 6144], P(('dp', 'slab'), 'mp')
- g_out: float32 [2048, 3072], P(('dp', 'mp'), 'slab')
- g_embed: float32 [64, 3072], P('dp', 'mp')
The draws below stay inside these ranges and needn't reach their ends.
Inputs may be any that keep to these rules, and one draw needn't show every extreme that they name: `clip_frames`: frames of each clip; they sum to 64 and the longest has exactly 32. `clip_res`: even latent heights and widths; some clip has the full 16 x 16 grid. `token_place`: a permutation of the 4096 positions.
All inputs are finite; a program needn't handle non-finite values.
Results may differ from the reference program's by a relative error of at most 0.024.
Values may be sent and summed in bfloat16 or wider, within the bound.
No kernel may reach another device: no remote copies, remote signals or barrier semaphores. Data moves between devices by JAX's collectives and lax.ppermute only.
A program may use at most 128 MiB of HBM per device.

```python
import math
import jax
import jax.numpy as jnp
import numpy as np
from jax import lax

D = 3072
HD = 128
H = 16
C = 512
LAT = 16
GROUPS = 32
CLIPS = 4
SIDE = 16
F = 64
PSIDE = 8
CELLS = 256
GS = 16
TOK = 4096
N_SLAB = 16
N_MP = 8


def draw_enc_feat(key, part):
    key = jax.random.fold_in(key, 11)
    base_key = jax.random.fold_in(key, 0)
    chan_key = jax.random.fold_in(key, 1)
    cell_key = jax.random.fold_in(key, 2)
    jitter_key = jax.random.fold_in(key, 4)
    frame_off_key = jax.random.fold_in(key, 5)
    chan_off_key = jax.random.fold_in(key, 6)
    frame_pos = jnp.arange(F, dtype=jnp.float32)
    ramp = jnp.exp(math.log(3.0) * (frame_pos / max(F - 1, 1) - 0.5))
    jitter = jnp.exp(jax.random.uniform(jitter_key, (F,), jnp.float32, -1.25, 1.25))
    chan_scale = jnp.exp(jax.random.uniform(chan_key, (C,), jnp.float32, math.log(0.3), math.log(2.0)))
    cell_scale = jnp.exp(jax.random.uniform(cell_key, (CELLS,), jnp.float32, -0.85, 0.85))
    frame_scale = ramp * jitter
    scale_all = frame_scale[:, None, None] * chan_scale[None, :, None] * cell_scale[None, None, :]
    frame_off = jax.random.uniform(frame_off_key, (F, 1, 1), jnp.float32, -1.0, 1.0)
    chan_off = jax.random.uniform(chan_off_key, (F, C, 1), jnp.float32, -1.0, 1.0)
    offset = 0.7 * frame_off + 0.3 * chan_off
    rough = jnp.clip(jax.random.normal(base_key, (F, C, CELLS), jnp.float32), -3.0, 3.0)
    values = (rough + offset) * scale_all
    return values.astype(jnp.bfloat16)


def draw_clip_res(key, part):
    key = jax.random.fold_in(key, 23)
    size_key, pick_key = jax.random.split(key)
    halves = jax.random.randint(size_key, (CLIPS, 2), SIDE // 4, SIDE // 2 + 1)
    chosen = jax.random.randint(pick_key, (), 0, CLIPS)
    full_clip = jnp.arange(CLIPS)[:, None] == chosen
    return jnp.where(full_clip, SIDE, 2 * halves).astype(jnp.int32)


def levels(rng, extent, shards, low, top_value):
    def one(axis_at, blocks):
        steps = jax.random.uniform(jax.random.fold_in(jax.random.fold_in(rng, 6), axis_at), (blocks,), jnp.float32, low / len(shards), top_value / len(shards))
        return jnp.repeat(jnp.exp(steps), extent[axis_at] // blocks).reshape((-1,) + (1,) * (len(extent) - axis_at - 1))

    gain = one(*shards[0])
    for cut in shards[1:]:
        gain = gain * one(*cut)
    return gain


def profile(count, total, reach, slope):
    weights = [(1 << 20) // math.isqrt(grade ** slope) + 1 for grade in range(2, count + 1)]
    spare, holding = total - reach - (count - 1), [1] * (count - 1)
    while spare > 0:
        free = [i for i in range(count - 1) if holding[i] < reach]
        pool, left = sum([weights[i] for i in free]), spare
        for i in free:
            addition = min(reach - holding[i], max(1, left * weights[i] // pool), spare)
            holding[i] = holding[i] + addition
            spare = spare - addition
    return np.array([reach] + holding)


def ragged(key, count, total, bound, lean):
    if count == 2:
        one = jax.random.randint(key, (), max(1, total - bound), min(bound, total - 1) + 1)
        return jnp.stack([one, total - one])
    tallies = jnp.asarray(profile(count, total, bound, lean), jnp.int32)
    pairs = (count - 1) // 2
    donor, receiver = tallies[1:1 + 2 * pairs:2], tallies[2:2 + 2 * pairs:2]
    room = jnp.minimum(donor - 1, bound - receiver)
    moved = jax.random.randint(jax.random.fold_in(key, 1), (pairs,), 0, 1 << 20) % (room + 1)
    tallies = tallies.at[1:1 + 2 * pairs:2].set(donor - moved).at[2:2 + 2 * pairs:2].set(receiver + moved)
    return tallies[jax.random.permutation(jax.random.fold_in(key, 2), count)]


def gaussian(own_key, extent, width, most, cuts=(), kind=jnp.bfloat16):
    drawn = jax.random.normal(own_key, extent, jnp.float32) * width
    if len(cuts) > 0:
        drawn = levels(own_key, extent, cuts, -0.22, 0.18) * drawn
    return jnp.clip(drawn, min=-most, max=most).astype(kind)


def setup_inputs(seed: int = 0, part: int = 0) -> dict:
    key_of = jax.random.split(jax.random.key(seed), 18)
    part_keys = jax.random.split(jax.random.fold_in(key_of[17], part), 18)
    enc_feat = draw_enc_feat(jax.random.fold_in(jax.random.fold_in(key_of[17], part), 71), part)
    gn_gain = jnp.clip(1.0 + 0.18 * jax.random.normal(key_of[1], (C,), jnp.float32), 0.1, 1.9)
    gn_bias = gaussian(key_of[2], (C,), 0.5, 3.0, ((0, 8),), jnp.float32)
    conv_w = gaussian(key_of[3], (C, 27 * LAT), (27 * C) ** -0.5, 0.0546875, ((0, 8),))
    clip_frames = ragged(part_keys[4], CLIPS, F, F // 2, 1).astype(jnp.int32)
    clip_res = draw_clip_res(jax.random.fold_in(jax.random.fold_in(key_of[17], part), 71), part)
    token_place = jax.random.permutation(part_keys[6], TOK).astype(jnp.int32)
    embed_w = gaussian(key_of[7], (4 * LAT, D), (4 * LAT) ** -0.5, 0.75)
    embed_b = gaussian(key_of[8], (D,), 0.5, 3.0, (), jnp.float32)
    mod_shift = gaussian(part_keys[9], (D,), 0.5, 3.0, (), jnp.float32)
    mod_scale = gaussian(part_keys[10], (D,), 0.3, 2.0, (), jnp.float32)
    mod_gate = gaussian(part_keys[11], (D,), 1.0, 4.0, (), jnp.float32)
    w_qkv = gaussian(key_of[12], (D, 3 * H * HD), D ** -0.5, 0.109375, ((1, 8),))
    q_gain = jnp.clip(1.0 + 0.18 * jax.random.normal(key_of[13], (HD,), jnp.float32), 0.1, 1.9)
    k_gain = jnp.clip(1.0 + 0.18 * jax.random.normal(key_of[14], (HD,), jnp.float32), 0.1, 1.9)
    w_out = gaussian(key_of[15], (H * HD, D), (H * HD) ** -0.5, 0.125, ((0, 8),))
    grad_out = gaussian(part_keys[16], (TOK, D), 1.0, 6.0, ((0, 16), (1, 8)))
    return dict(enc_feat=enc_feat, gn_gain=gn_gain, gn_bias=gn_bias, conv_w=conv_w, clip_frames=clip_frames, clip_res=clip_res, token_place=token_place, embed_w=embed_w, embed_b=embed_b, mod_shift=mod_shift, mod_scale=mod_scale, mod_gate=mod_gate, w_qkv=w_qkv, q_gain=q_gain, k_gain=k_gain, w_out=w_out, grad_out=grad_out)


EPSILON = 1e-06
HIGHEST = lax.Precision.HIGHEST

def rounded(values):
    return lax.optimization_barrier(values.astype(jnp.bfloat16)).astype(jnp.float32)

def rms_scale(values):
    return lax.rsqrt(lax.optimization_barrier(jnp.mean(values * values, axis=-1, keepdims=True)) + EPSILON)

def rms_back(grad_hat, normed, inverse, weight):
    scaled = grad_hat * weight
    return inverse * (scaled - normed * lax.optimization_barrier(jnp.mean(scaled * normed, axis=-1, keepdims=True)))

def reference(enc_feat, gn_gain, gn_bias, conv_w, clip_frames, clip_res, token_place, embed_w, embed_b, mod_shift, mod_scale, mod_gate, w_qkv, q_gain, k_gain, w_out, grad_out):
    clip_ends = jnp.cumsum(clip_frames).astype(jnp.int32)
    clip_starts = (clip_ends - clip_frames).astype(jnp.int32)
    frame_id = jnp.arange(F, dtype=jnp.int32)
    clip_of = lax.optimization_barrier(jnp.sum((frame_id[:, None] >= clip_ends[None, :]).astype(jnp.int32), axis=1)).astype(jnp.int32)
    height = clip_res[clip_of, 0]
    width_of = clip_res[clip_of, 1]
    start_of = clip_starts[clip_of]
    cell_id = jnp.arange(CELLS, dtype=jnp.int32)
    valid = ((cell_id[None, :] // SIDE < height[:, None]) & (cell_id[None, :] % SIDE < width_of[:, None])).astype(jnp.float32)
    features = enc_feat.astype(jnp.float32).reshape(F, GROUPS, GS, CELLS)
    masked = features * valid[:, None, None, :]
    member = (clip_of[:, None] == jnp.arange(CLIPS, dtype=jnp.int32)[None, :]).astype(jnp.float32)
    group_sum = jnp.dot(member.T, lax.optimization_barrier(jnp.sum(masked, axis=(2, 3))), precision=HIGHEST)
    group_sq = jnp.dot(member.T, lax.optimization_barrier(jnp.sum(masked * features, axis=(2, 3))), precision=HIGHEST)
    counts = (clip_frames * clip_res[:, 0] * clip_res[:, 1] * GS).astype(jnp.float32)
    group_mean = group_sum / counts[:, None]
    group_rstd = lax.rsqrt(group_sq / counts[:, None] - group_mean * group_mean + EPSILON)
    normed = (features - group_mean[clip_of][:, :, None, None]) * group_rstd[clip_of][:, :, None, None]
    activated = jax.nn.silu(normed.reshape(F, C, CELLS) * gn_gain[None, :, None] + gn_bias[None, :, None]) * valid[:, None, :]
    activated = activated.astype(jnp.bfloat16)
    projected = jnp.einsum('fin,ik->fkn', activated.astype(jnp.float32), conv_w.astype(jnp.float32), precision=HIGHEST)
    tap_table = projected.reshape(F, 3, 3, 3, LAT, SIDE, SIDE)
    conv_sum = jnp.zeros((F, LAT, SIDE, SIDE), jnp.float32)
    for step_t in range(3):
        source = jnp.maximum(frame_id - 2 + step_t, start_of)
        padded = jnp.pad(tap_table[source, step_t], ((0, 0), (0, 0), (0, 0), (0, 0), (1, 1), (1, 1)))
        for step_y in range(3):
            for step_x in range(3):
                conv_sum = conv_sum + padded[:, step_y, step_x, :, step_y:step_y + SIDE, step_x:step_x + SIDE]
    latents = conv_sum.reshape(F, LAT, CELLS)
    patches = latents.reshape(F, LAT, PSIDE, 2, PSIDE, 2).transpose(0, 2, 4, 1, 3, 5).reshape(TOK, 4 * LAT).astype(jnp.bfloat16)
    patch_id = jnp.arange(PSIDE, dtype=jnp.int32)
    tok_valid = ((2 * patch_id[None, :, None] < height[:, None, None]) & (2 * patch_id[None, None, :] < width_of[:, None, None])).astype(jnp.int32).reshape(TOK)
    tok_code = ((jnp.repeat(clip_of, PSIDE * PSIDE) + 1) * 2 + tok_valid).astype(jnp.int32)
    sequence = jnp.zeros((TOK, 4 * LAT), jnp.bfloat16).at[token_place].set(patches)
    seq_code = jnp.zeros((TOK,), jnp.int32).at[token_place].set(tok_code)
    hidden = (jnp.dot(sequence, embed_w, preferred_element_type=jnp.float32) + embed_b).astype(jnp.bfloat16)
    hidden_f = hidden.astype(jnp.float32)
    centered = hidden_f - lax.optimization_barrier(jnp.mean(hidden_f, axis=-1, keepdims=True))
    ln_rstd = lax.rsqrt(lax.optimization_barrier(jnp.mean(centered * centered, axis=-1, keepdims=True)) + EPSILON)
    xnorm = centered * ln_rstd
    modded = (xnorm * (1.0 + mod_scale) + mod_shift).astype(jnp.bfloat16)
    qkv_out = jnp.dot(modded, w_qkv, preferred_element_type=jnp.float32).reshape(TOK, H, 3, HD)
    q_inv = rms_scale(qkv_out[:, :, 0])
    q_norm = qkv_out[:, :, 0] * q_inv
    k_inv = rms_scale(qkv_out[:, :, 1])
    k_norm = qkv_out[:, :, 1] * k_inv
    queries = (q_norm * q_gain).astype(jnp.bfloat16)
    keys_all = (k_norm * k_gain).astype(jnp.bfloat16)
    values = qkv_out[:, :, 2].astype(jnp.bfloat16)
    allowed = (seq_code[None, :] // 2 == seq_code[:, None] // 2) & (seq_code[None, :] % 2 == 1)
    score_scale = HD ** (-0.5)

    def forward_head(operands):
        query_h, key_h, value_h = operands
        scores = jnp.dot(query_h, key_h.T, preferred_element_type=jnp.float32) * score_scale
        masked_s = jnp.where(allowed, scores, -1e+30)
        row_top = lax.optimization_barrier(jnp.max(masked_s, axis=-1, keepdims=True))
        log_total = row_top[:, 0] + jnp.log(lax.optimization_barrier(jnp.sum(jnp.exp(masked_s - row_top), axis=-1)))
        weights = jnp.exp(jnp.where(allowed, scores - log_total[:, None], -1e+30))
        result = jnp.dot(weights.astype(jnp.bfloat16), value_h, preferred_element_type=jnp.float32)
        return (result.astype(jnp.bfloat16), log_total)
    head_q = jnp.swapaxes(queries, 0, 1)
    head_k = jnp.swapaxes(keys_all, 0, 1)
    head_v = jnp.swapaxes(values, 0, 1)
    outputs, log_totals = lax.map(forward_head, (head_q, head_k, head_v))
    attended = jnp.swapaxes(outputs, 0, 1)
    flat_heads = attended.reshape(TOK, H * HD)
    group_cols = H * HD // N_MP
    attn_sum = jnp.zeros((TOK, D), jnp.float32)
    for group_num in range(N_MP):
        col_first = group_num * group_cols
        attn_sum = attn_sum + rounded(jnp.dot(flat_heads[:, col_first:col_first + group_cols], w_out[col_first:col_first + group_cols], preferred_element_type=jnp.float32))
    block_out = (hidden_f + mod_gate * attn_sum).astype(jnp.bfloat16)
    cotangent = grad_out.astype(jnp.float32)
    d_attn = (mod_gate * cotangent).astype(jnp.bfloat16)
    shard_rows = TOK // N_SLAB
    g_out = jnp.zeros((H * HD, D), jnp.float32)
    for shard_num in range(N_SLAB):
        row_first = shard_num * shard_rows
        g_out = g_out + rounded(jnp.dot(flat_heads[row_first:row_first + shard_rows].T, d_attn[row_first:row_first + shard_rows], preferred_element_type=jnp.float32))
    d_out = jnp.dot(d_attn, w_out.T, preferred_element_type=jnp.float32).astype(jnp.bfloat16).reshape(TOK, H, HD)
    delta_rows = lax.optimization_barrier(jnp.sum(d_out.astype(jnp.float32) * attended.astype(jnp.float32), axis=-1))

    def backward_head(operands):
        query_h, key_h, value_h, dout_h, lse_h, delta_h = operands
        scores = jnp.dot(query_h, key_h.T, preferred_element_type=jnp.float32) * score_scale
        weights = jnp.exp(jnp.where(allowed, scores - lse_h[:, None], -1e+30))
        d_prob = jnp.dot(dout_h, value_h.T, preferred_element_type=jnp.float32)
        d_score = (weights * (d_prob - delta_h[:, None])).astype(jnp.bfloat16)
        grad_q = jnp.dot(d_score, key_h, preferred_element_type=jnp.float32) * score_scale
        grad_k = jnp.dot(d_score.T, query_h, preferred_element_type=jnp.float32) * score_scale
        grad_v = jnp.dot(weights.astype(jnp.bfloat16).T, dout_h, preferred_element_type=jnp.float32)
        return (grad_q, grad_k, grad_v)
    grad_q, grad_k, grad_v = lax.map(backward_head, (head_q, head_k, head_v, jnp.swapaxes(d_out, 0, 1), log_totals, delta_rows.T))
    dq_raw = rms_back(jnp.swapaxes(grad_q, 0, 1), q_norm, q_inv, q_gain)
    dk_raw = rms_back(jnp.swapaxes(grad_k, 0, 1), k_norm, k_inv, k_gain)
    d_qkv = jnp.stack([dq_raw, dk_raw, jnp.swapaxes(grad_v, 0, 1)], axis=2).reshape(TOK, 3 * H * HD).astype(jnp.bfloat16)
    g_qkv = jnp.zeros((D, 3 * H * HD), jnp.float32)
    for shard_num in range(N_SLAB):
        row_first = shard_num * shard_rows
        g_qkv = g_qkv + rounded(jnp.dot(modded[row_first:row_first + shard_rows].T, d_qkv[row_first:row_first + shard_rows], preferred_element_type=jnp.float32))
    qkv_cols = 3 * H * HD // N_MP
    d_mod = jnp.zeros((TOK, D), jnp.float32)
    for group_num in range(N_MP):
        col_first = group_num * qkv_cols
        d_mod = d_mod + rounded(jnp.dot(d_qkv[:, col_first:col_first + qkv_cols], w_qkv[:, col_first:col_first + qkv_cols].T, preferred_element_type=jnp.float32))
    d_norm = d_mod * (1.0 + mod_scale)
    d_hidden = cotangent + ln_rstd * (d_norm - lax.optimization_barrier(jnp.mean(d_norm, axis=-1, keepdims=True)) - xnorm * lax.optimization_barrier(jnp.mean(d_norm * xnorm, axis=-1, keepdims=True)))
    g_embed = jnp.dot(sequence.astype(jnp.float32).T, d_hidden, precision=HIGHEST)
    return (latents, block_out, g_qkv, g_out, g_embed)
```

```python
import functools

import jax
import jax.numpy as jnp
from jax import lax
from jax.experimental import pallas as pl
from jax.experimental.pallas import tpu as pltpu
from jax.sharding import PartitionSpec as P

D = 3072
HD = 128
LAT = 16
CLIPS = 4
SIDE = 16
PSIDE = 8
CELLS = 256
GS = 16
HEADS = 2
ROWS = 256
FRAMES = 4
FEAT = 64
AUG = 80
EXT = 144
EPSILON = 1e-06
HIGHEST = lax.Precision.HIGHEST
LOG2E = 1.4426950408889634
OFF = -1e30
F32 = jnp.float32
BF16 = jnp.bfloat16
VMEM_BYTES = 50 * 1024 * 1024


def nn(a, b):
    return lax.dot_general(a, b, (((1,), (0,)), ((), ())), preferred_element_type=F32)


def nt(a, b):
    return lax.dot_general(a, b, (((1,), (1,)), ((), ())), preferred_element_type=F32)


def tn(a, b):
    return lax.dot_general(a, b, (((0,), (0,)), ((), ())), preferred_element_type=F32)


def hi_lo(value):
    hi = value.astype(BF16)
    return hi, (value - hi.astype(F32)).astype(BF16)


def clip_number(meta, frame):
    one = meta[0]
    two = one + meta[1]
    three = two + meta[2]
    return (
        jnp.where(frame >= one, 1, 0) + jnp.where(frame >= two, 1, 0) + jnp.where(frame >= three, 1, 0)
    )


def frame_facts(meta, frame):
    clip = clip_number(meta, frame)
    one = meta[0]
    two = one + meta[1]
    three = two + meta[2]
    start = jnp.where(
        clip == 0, 0, jnp.where(clip == 1, one, jnp.where(clip == 2, two, three))
    )
    return clip, start, meta[4 + 2 * clip], meta[5 + 2 * clip]


def cell_valid(height, width):
    cell = lax.broadcasted_iota(jnp.int32, (1, CELLS), 1)
    return ((cell >> 4) < height) & ((cell & 15) < width)


def stats_kernel(meta, enc, place, out):
    lane = lax.broadcasted_iota(jnp.int32, (FEAT, 128), 1)
    total = jnp.zeros((FEAT, 128), F32)
    for f in range(FRAMES):
        clip, _, height, width = frame_facts(meta, meta[12] * FRAMES + f)
        kept = jnp.where(cell_valid(height, width), enc[f].astype(F32), 0.0)
        sums = jnp.sum(kept, axis=1, keepdims=True)
        squares = jnp.sum(kept * kept, axis=1, keepdims=True)
        total = total + jnp.where(lane == clip, sums, 0.0) + jnp.where(lane == clip + 4, squares, 0.0)
    for g in range(4):
        out[g : g + 1, :] = jnp.sum(total[g * GS : (g + 1) * GS], axis=0, keepdims=True)
    out[4:6, :] = place[...].astype(F32)
    out[6:8, :] = jnp.zeros((2, 128), F32)


def conv_kernel(meta, enc, rim, sums, gain, bias, taps, spread, out, proj):
    totals = jnp.sum(sums[...], axis=0)
    lane = lax.broadcasted_iota(jnp.int32, (8, 128), 1)
    first = meta[12] * FRAMES
    cell = lax.broadcasted_iota(jnp.int32, (1, CELLS), 1)
    row, col = cell >> 4, cell & 15
    for j in range(FRAMES + 2):
        clip, _, height, width = frame_facts(meta, jnp.maximum(first - 2 + j, 0))
        count = (meta[clip] * height * width * GS).astype(F32)
        mean = jnp.sum(jnp.where(lane == clip, totals, 0.0), axis=1, keepdims=True) / count
        square = jnp.sum(jnp.where(lane == clip + 4, totals, 0.0), axis=1, keepdims=True) / count
        rstd = lax.rsqrt(square - mean * mean + EPSILON)
        mean_c = jnp.concatenate([jnp.broadcast_to(mean[g : g + 1], (GS, 1)) for g in range(4)], axis=0)
        rstd_c = jnp.concatenate([jnp.broadcast_to(rstd[g : g + 1], (GS, 1)) for g in range(4)], axis=0)
        value = rim[j] if j < 2 else enc[j - 2]
        pre = (value.astype(F32) - mean_c) * rstd_c * gain[...] + bias[...]
        act = jnp.where(cell_valid(height, width), pre / (1.0 + jnp.exp(-pre)), 0.0)
        proj[j] = nn(taps[...], act.astype(BF16))
    frames = []
    for f in range(FRAMES):
        _, start, _, _ = frame_facts(meta, first + f)
        source = [jnp.maximum(first + f - 2 + dt, start) - first + 2 for dt in range(3)]
        planes = [proj[source[dt], dt * 144 : (dt + 1) * 144, :] for dt in range(3)]
        joint = planes[0] + planes[1] + planes[2]
        result = jnp.zeros((LAT, CELLS), F32)
        for dx in range(3):
            part = jnp.zeros((LAT, CELLS), F32)
            for dy in range(3):
                tap = (dy * 3 + dx) * LAT
                piece = joint[tap : tap + LAT]
                if dy != 1:
                    piece = pltpu.roll(piece, (-(dy - 1) * SIDE) % CELLS, 1)
                    inside = (row >= 1) if dy == 0 else (row <= SIDE - 2)
                    piece = jnp.where(inside, piece, 0.0)
                part = part + piece
            if dx != 1:
                part = pltpu.roll(part, (-(dx - 1)) % CELLS, 1)
                inside = (col >= 1) if dx == 0 else (col <= SIDE - 2)
                part = jnp.where(inside, part, 0.0)
            result = result + part
        frames.append(result.astype(BF16))
    sorted_cells = nn(jnp.concatenate(frames, axis=0), spread[...]).astype(BF16)
    for ab in range(4):
        out[ab * LAT : (ab + 1) * LAT, :] = jnp.concatenate(
            [
                sorted_cells[f * LAT : (f + 1) * LAT, ab * 64 : (ab + 1) * 64]
                for f in range(FRAMES)
            ],
            axis=1,
        )


def shift_row(m_hi, m_lo, part):
    unit = jnp.where(lax.broadcasted_iota(jnp.int32, (16, AUG), 1) == FEAT + 1, 1.0, 0.0).astype(BF16)
    return (nt(unit, m_hi[part, :]) + nt(unit, m_lo[part, :]))[0:1]


def attn_kernel(
    meta,
    patches,
    place,
    gram_hi,
    gram_lo,
    m_cat,
    m_hi,
    m_lo,
    d_out,
    q_gain,
    k_gain,
    grad_out,
    sums,
    attended,
    own,
    k_t,
    v_t,
    s_t,
    kn_t,
    rk_t,
    prob,
):
    blocks = patches.shape[0]
    row_aug = lax.broadcasted_iota(jnp.int32, (AUG, ROWS), 0)
    row16 = lax.broadcasted_iota(jnp.int32, (16, ROWS), 0)
    token = lax.broadcasted_iota(jnp.int32, (1, ROWS), 1)
    position = lax.broadcasted_iota(jnp.int32, (ROWS, ROWS), 0).astype(F32)
    base = (meta[12] * ROWS).astype(F32)
    one_row = jnp.where(row16 == 0, 1.0, 0.0).astype(BF16)
    two_rows = jnp.where(row16 <= 1, 1.0, 0.0).astype(BF16)

    def lanes(j):
        return pl.ds(pl.multiple_of(j * ROWS, ROWS), ROWS)

    def prepare(j, carry):
        x_q, clip_q = carry
        block = lanes(j)
        raw = patches[j]
        x_aug = jnp.concatenate([raw, one_row], axis=0)
        x_f = x_aug.astype(F32)
        gx = nn(gram_hi[...], x_aug) + nn(gram_lo[...], x_aug)
        rstd = lax.rsqrt(jnp.sum(gx * x_f, axis=0, keepdims=True) + EPSILON)
        s = jnp.where(row_aug == FEAT + 1, 1.0, x_f * rstd)
        s_hi, s_lo = hi_lo(s)
        s_t[:, block] = s_hi
        s_cat = jnp.concatenate([s_hi, s_lo, s_hi], axis=0)
        frame = j * FRAMES + (token >> 6)
        clip = clip_number(meta, frame)
        height = jnp.zeros((1, ROWS), jnp.int32)
        width = jnp.zeros((1, ROWS), jnp.int32)
        for c in range(CLIPS):
            height = jnp.where(clip == c, meta[4 + 2 * c], height)
            width = jnp.where(clip == c, meta[5 + 2 * c], width)
        valid = (2 * ((token >> 3) & 7) < height) & (2 * (token & 7) < width)
        member = row16 == clip
        mask = jnp.where((row16 < CLIPS) & ~(member & valid), OFF, 0.0).astype(BF16)
        for h in range(HEADS):
            kv = nn(m_cat[h * 384 + 128 : h * 384 + 384, :], s_cat)
            k = kv[:HD]
            rk = lax.rsqrt(jnp.mean(k * k, axis=0, keepdims=True) + EPSILON)
            kn = k * rk
            kn_t[h, :, block] = kn
            rk_t[h, :, block] = jnp.broadcast_to(rk, (8, ROWS))
            k_t[h, :HD, block] = (kn * k_gain[...]).astype(BF16)
            k_t[h, HD:, block] = mask
            v_t[h, :HD, block] = kv[HD:].astype(BF16)
            v_t[h, HD:, block] = two_rows
        spot = jnp.concatenate([place[j, 4:5, :], place[j, 5:6, :]], axis=1)
        chosen = jnp.where(spot == position + base, 1.0, 0.0).astype(BF16)
        x_q = x_q + nt(chosen, x_aug)
        clip_q = clip_q + nt(chosen, jnp.where(member, 1.0, 0.0).astype(BF16))
        return x_q, clip_q

    x_q, clip_q = lax.fori_loop(
        0, blocks, prepare, (jnp.zeros((ROWS, AUG), F32), jnp.zeros((ROWS, 16), F32))
    )
    x_qb = x_q.astype(BF16)
    own[...] = x_qb
    sums[:, 896:1280] = tn(x_qb, grad_out[...])
    gx_q = nn(x_qb, gram_hi[...]) + nn(x_qb, gram_lo[...])
    rstd_q = lax.rsqrt(jnp.sum(gx_q * x_q, axis=1, keepdims=True) + EPSILON)
    lane_aug = lax.broadcasted_iota(jnp.int32, (ROWS, AUG), 1)
    s_q = jnp.where(lane_aug == FEAT + 1, 1.0, x_q * rstd_q)
    s_qhi, s_qlo = hi_lo(s_q)
    lane16 = lax.broadcasted_iota(jnp.int32, (ROWS, 16), 1)

    q_ext, q_ext_t, do_ext, do_ext_t, q_keep = [], [], [], [], []
    for h in range(HEADS):
        mine = slice(h * 384, h * 384 + 128)
        q = nt(s_qhi, m_hi[mine, :]) + nt(s_qlo, m_hi[mine, :]) + nt(s_qhi, m_lo[mine, :])
        rq = lax.rsqrt(jnp.mean(q * q, axis=1, keepdims=True) + EPSILON)
        qn = q * rq
        qb = (qn * (q_gain[...] * (HD**-0.5 * LOG2E))).astype(BF16)
        q_keep.append((q, rq, qn))
        q_ext.append(jnp.concatenate([qb, clip_q.astype(BF16)], axis=1))
        ones = jnp.where(lane16 == 0, 1.0, 0.0)
        q_ext_t.append(jnp.concatenate([qb.astype(F32), ones], axis=1).T.astype(BF16))

        def forward(j, total, h=h):
            block = lanes(j)
            p = jnp.exp2(nn(q_ext[h], k_t[h, :, block])).astype(BF16)
            prob[h, :, block] = p
            return total + nt(p, v_t[h, :, block])

        total = lax.fori_loop(0, blocks, forward, jnp.zeros((ROWS, EXT), F32))
        inv_l = 1.0 / total[:, HD : HD + 1]
        att = (total[:, :HD] * inv_l).astype(BF16)
        attended[:, h * HD : (h + 1) * HD] = att
        do = d_out[:, h * HD : (h + 1) * HD].astype(F32)
        delta = jnp.sum(do * att.astype(F32), axis=1, keepdims=True)
        shift_v = shift_row(m_hi, m_lo, slice(h * 384 + 256, h * 384 + 384))
        weight = (delta - jnp.sum(do * shift_v, axis=1, keepdims=True)) * inv_l
        scaled = (do * inv_l).astype(BF16)
        d_hi, d_lo = hi_lo(-delta * inv_l)
        extra = jnp.where(lane16 == 0, d_hi.astype(F32), jnp.where(lane16 == 1, d_lo.astype(F32), 0.0))
        do_ext.append(jnp.concatenate([scaled, extra.astype(BF16)], axis=1))
        w_hi, w_lo = hi_lo(weight)
        extra = jnp.where(lane16 == 0, w_hi.astype(F32), jnp.where(lane16 == 1, w_lo.astype(F32), 0.0))
        do_ext_t.append(jnp.concatenate([scaled.astype(F32), extra], axis=1).T.astype(BF16))

    def backward(j, carry):
        quad, per_head = carry
        block = lanes(j)
        s_block = s_t[:, block]
        m2 = jnp.zeros((1, ROWS), F32)
        done = []
        for h in range(HEADS):
            grad_q, p_k, p_v = per_head[h]
            pb = prob[h, :, block]
            d_score = (pb.astype(F32) * nn(do_ext[h], v_t[h, :, block])).astype(BF16)
            grad_q = grad_q + nt(d_score, k_t[h, :HD, block])
            gk = nn(q_ext_t[h], d_score)
            gv = nn(do_ext_t[h], pb)
            kn = kn_t[h, :, block]
            rk = rk_t[h, 0:1, block]
            scaled = gk[:HD] * (k_gain[...] * (1.0 / LOG2E))
            dk = rk * (scaled - kn * jnp.mean(scaled * kn, axis=0, keepdims=True))
            shift_k = m_hi[h * 384 + 128 : h * 384 + 256, FEAT + 1 : FEAT + 2].astype(F32) + m_lo[
                h * 384 + 128 : h * 384 + 256, FEAT + 1 : FEAT + 2
            ].astype(F32)
            m2 = m2 + jnp.sum(dk * (kn * (1.0 / rk) - shift_k), axis=0, keepdims=True)
            m2 = m2 + gk[HD : HD + 1] + gv[HD : HD + 1] + gv[HD + 1 : HD + 2]
            p_k = p_k + nt(s_block, dk.astype(BF16))
            p_v = p_v + nt(s_block, gv[:HD].astype(BF16))
            done.append((grad_q, p_k, p_v))
        quad = quad + nt((s_block.astype(F32) * m2).astype(BF16), s_block)
        return quad, tuple(done)

    zero = (jnp.zeros((ROWS, HD), F32), jnp.zeros((AUG, HD), F32), jnp.zeros((AUG, HD), F32))
    quad, per_head = lax.fori_loop(
        0, blocks, backward, (jnp.zeros((AUG, AUG), F32), (zero,) * HEADS)
    )
    m2_q = jnp.zeros((ROWS, 1), F32)
    for h in range(HEADS):
        grad_q, p_k, p_v = per_head[h]
        q, rq, qn = q_keep[h]
        scaled = grad_q * (q_gain[...] * HD**-0.5)
        dq = rq * (scaled - qn * jnp.mean(scaled * qn, axis=1, keepdims=True))
        mine = slice(h * 384, h * 384 + 128)
        shift_q = shift_row(m_hi, m_lo, mine)
        m2_q = m2_q + jnp.sum(dq * (q - shift_q), axis=1, keepdims=True)
        sums[:, h * 384 : h * 384 + 128] = tn(s_qhi, dq.astype(BF16))
        sums[:, h * 384 + 128 : h * 384 + 256] = p_k
        sums[:, h * 384 + 256 : h * 384 + 384] = p_v
    quad = (quad + tn((s_q * m2_q).astype(BF16), s_qhi)) * (1.0 / D)
    sums[:, 768:896] = jnp.concatenate([quad, jnp.zeros((AUG, 128 - AUG), F32)], axis=1)


VMEM = pl.BlockSpec(memory_space=pltpu.VMEM)
SMEM = pl.BlockSpec(memory_space=pltpu.SMEM)


def call(kernel, inputs, outputs, scratch, flops):
    return pl.pallas_call(
        kernel,
        out_shape=outputs,
        in_specs=[SMEM] + [VMEM] * (len(inputs) - 1),
        out_specs=jax.tree.map(lambda _: VMEM, outputs),
        scratch_shapes=scratch,
        compiler_params=pltpu.CompilerParams(vmem_limit_bytes=VMEM_BYTES),
        cost_estimate=pl.CostEstimate(flops=flops, bytes_accessed=1 << 20, transcendentals=0),
    )(*inputs)


def shift_by(value, axis, move):
    return lax.ppermute(value, axis, [(i, move(i)) for i in range(lax.axis_size(axis))])


def along_x(k):
    return lambda i: (i // 4) * 4 + (i % 4 + k) % 4


def along_y(k):
    return lambda i: ((i // 4 + k) % 4) * 4 + i % 4


def along_z(k):
    return lambda i: ((i // 2 + k) % 4) * 2 + i % 2


def sum_of_four(value, axis, move, kind):
    sent = value.astype(kind)
    one, two, three = (shift_by(sent, axis, move(k)).astype(F32) for k in (1, 2, 3))
    return (sent.astype(F32) + two) + (one + three)


def body(
    enc_feat,
    gn_gain,
    gn_bias,
    conv_w,
    clip_frames,
    clip_res,
    token_place,
    embed_w,
    embed_b,
    mod_shift,
    mod_scale,
    mod_gate,
    w_qkv,
    q_gain,
    k_gain,
    w_out,
    grad_out,
):
    slabs = lax.axis_size("slab")
    slab_pos = lax.axis_index("slab").astype(jnp.int32)
    mp_size = lax.axis_size("mp")
    mp_pos = lax.axis_index("mp")
    cols_dev = D // mp_size
    col_first = mp_pos * cols_dev
    row_cols = D // slabs

    meta = jnp.concatenate(
        [clip_frames, clip_res.reshape(-1), slab_pos[None], jnp.zeros((3,), jnp.int32)]
    )
    rim = shift_by(enc_feat[FRAMES - 2 :], "slab", lambda i: (i + 1) % slabs)
    stats = call(
        stats_kernel,
        (meta, enc_feat, token_place.reshape(2, 128)),
        jax.ShapeDtypeStruct((8, 128), F32),
        [],
        1 << 20,
    )
    all_stats = lax.all_to_all(
        jnp.broadcast_to(stats, (slabs, 8, 128)), "slab", split_axis=0, concat_axis=0, tiled=True
    )
    cell = jnp.arange(CELLS, dtype=jnp.int32)
    row, col = cell // SIDE, cell % SIDE
    sorted_place = ((row % 2) * 2 + col % 2) * 64 + (row // 2) * PSIDE + col // 2
    spread = (sorted_place[:, None] == cell[None, :]).astype(BF16)
    partial = call(
        conv_kernel,
        (
            meta,
            enc_feat,
            rim,
            all_stats,
            gn_gain[:, None],
            gn_bias[:, None],
            conv_w.T,
            spread,
        ),
        jax.ShapeDtypeStruct((FEAT, CELLS), BF16),
        [pltpu.VMEM((FRAMES + 2, 432, CELLS), F32)],
        1 << 28,
    )
    other = shift_by(partial, "mp", lambda i: i ^ 1)
    pair = partial.astype(F32) + other.astype(F32)
    lat_sorted = sum_of_four(pair, "mp", along_z, BF16)
    patches = lat_sorted.astype(BF16)
    all_patches = lax.all_to_all(
        jnp.broadcast_to(patches, (slabs, FEAT, CELLS)), "slab", split_axis=0, concat_axis=0, tiled=True
    )
    latents = (
        lat_sorted.reshape(2, 2, LAT, FRAMES, PSIDE, PSIDE)
        .transpose(3, 2, 4, 0, 5, 1)
        .reshape(FRAMES, LAT, CELLS)
    )

    embed_f = embed_w.astype(F32).reshape(LAT, 4, D).transpose(1, 0, 2).reshape(FEAT, D)
    embed_aug = jnp.concatenate([embed_f, embed_b[None]], axis=0)
    centered = embed_aug - jnp.mean(embed_aug, axis=1, keepdims=True)
    gram = lax.dot_general(centered, centered, (((1,), (1,)), ((), ())), precision=HIGHEST) / D
    gram_hi, gram_lo = hi_lo(jnp.pad(gram, ((0, AUG - 65), (0, AUG - 65))))
    modulated = jnp.concatenate(
        [centered * (1.0 + mod_scale), mod_shift[None], jnp.zeros((AUG - 66, D), F32)], axis=0
    )
    mod_hi, mod_lo = hi_lo(modulated)
    both = lax.dot_general(
        w_qkv,
        jnp.concatenate([mod_hi, mod_lo], axis=0),
        (((0,), (1,)), ((), ())),
        preferred_element_type=F32,
    )
    m_hi, m_lo = hi_lo(both[:, :AUG] + both[:, AUG:])
    m_cat = jnp.concatenate([m_hi, m_hi, m_lo], axis=1)

    cotangent = lax.all_gather(grad_out, "mp", axis=1, tiled=True)
    d_attn = (mod_gate * cotangent.astype(F32)).astype(BF16)
    d_out = nt(d_attn, w_out).astype(BF16)

    sums, attended, own = call(
        attn_kernel,
        (
            meta,
            all_patches,
            all_stats,
            gram_hi,
            gram_lo,
            m_cat,
            m_hi,
            m_lo,
            d_out,
            q_gain[None, :],
            k_gain[:, None],
            grad_out,
        ),
        (
            jax.ShapeDtypeStruct((AUG, 1280), F32),
            jax.ShapeDtypeStruct((ROWS, HEADS * HD), BF16),
            jax.ShapeDtypeStruct((ROWS, AUG), BF16),
        ),
        [
            pltpu.VMEM((HEADS, EXT, 4096), BF16),
            pltpu.VMEM((HEADS, EXT, 4096), BF16),
            pltpu.VMEM((AUG, 4096), BF16),
            pltpu.VMEM((HEADS, HD, 4096), F32),
            pltpu.VMEM((HEADS, 8, 4096), F32),
            pltpu.VMEM((HEADS, ROWS, 4096), BF16),
        ],
        1 << 33,
    )

    total = sum_of_four(sums, "slab", along_x, F32)
    total = sum_of_four(total, "slab", along_y, F32)
    own_rows = lax.dynamic_slice_in_dim(modulated, slab_pos * row_cols, row_cols, 1)
    g_qkv = lax.dot_general(
        own_rows[:66], total[:66, :768], (((0,), (0,)), ((), ())), precision=HIGHEST
    )
    back = nt(total[:FEAT, :768].astype(BF16), w_qkv) * (1.0 + mod_scale)
    back = back - jnp.mean(back, axis=1, keepdims=True)
    back = back - jnp.dot(total[:FEAT, 768 : 768 + 65], centered, precision=HIGHEST)
    pieces = back.astype(BF16).reshape(FEAT, mp_size, cols_dev).transpose(1, 0, 2)
    got = lax.all_to_all(pieces, "mp", split_axis=0, concat_axis=0, tiled=True)
    g_embed = jnp.sum(got.astype(F32), axis=0) + total[:FEAT, 896:1280]
    g_embed = g_embed.reshape(4, LAT, cols_dev).transpose(1, 0, 2).reshape(FEAT, cols_dev)

    attn_part = jnp.dot(attended, w_out, preferred_element_type=F32).astype(BF16)
    attn_got = lax.all_to_all(
        attn_part.reshape(ROWS, mp_size, cols_dev).transpose(1, 0, 2),
        "mp",
        split_axis=0,
        concat_axis=0,
        tiled=True,
    )
    attn_cols = jnp.sum(attn_got.astype(F32), axis=0)
    hidden_cols = (
        jnp.dot(
            own[:, :FEAT],
            lax.dynamic_slice_in_dim(embed_f.astype(BF16), col_first, cols_dev, 1),
            preferred_element_type=F32,
        )
        + lax.dynamic_slice_in_dim(embed_b, col_first, cols_dev, 0)
    ).astype(BF16)
    gate_cols = lax.dynamic_slice_in_dim(mod_gate, col_first, cols_dev, 0)
    block_out = (hidden_cols.astype(F32) + gate_cols * attn_cols).astype(BF16)
    g_part = tn(attended, d_attn).astype(BF16)
    g_got = lax.all_to_all(
        g_part.reshape(HEADS * HD, slabs, row_cols).transpose(1, 0, 2),
        "slab",
        split_axis=0,
        concat_axis=0,
        tiled=True,
    )
    g_out = jnp.sum(g_got.astype(F32), axis=0)
    return (latents, block_out, g_qkv, g_out, g_embed)


def solution(mesh):
    in_specs = (
        P(("dp", "slab"), "mp", None),
        P("mp"),
        P("mp"),
        P("mp", None),
        P("dp"),
        P("dp", None),
        P(("dp", "slab")),
        P(),
        P(),
        P("dp"),
        P("dp"),
        P("dp"),
        P(None, "mp"),
        P(),
        P(),
        P("mp", None),
        P(("dp", "slab"), "mp"),
    )
    out_specs = (
        P(("dp", "slab"), None, None),
        P(("dp", "slab"), "mp"),
        P(("dp", "slab"), "mp"),
        P(("dp", "mp"), "slab"),
        P("dp", "mp"),
    )
    return jax.shard_map(body, mesh=mesh, in_specs=in_specs, out_specs=out_specs, check_vma=False)
```

```python
import functools

import jax
import jax.numpy as jnp
from jax import lax
from jax.experimental import pallas as pl
from jax.experimental.pallas import tpu as pltpu
from jax.sharding import PartitionSpec as P

D = 3072
HD = 128
LAT = 16
CLIPS = 4
SIDE = 16
PSIDE = 8
CELLS = 256
GS = 16
HEADS = 2
ROWS = 256
FRAMES = 4
FEAT = 64
AUG = 80
EXT = 144
EPSILON = 1e-06
HIGHEST = lax.Precision.HIGHEST
LOG2E = 1.4426950408889634
OFF = -1e30
F32 = jnp.float32
BF16 = jnp.bfloat16
MIB = 1024 * 1024
PREPARE_UNROLL = 4
FWD_BLOCK = 1024
FWD_UNROLL = 1
BWD_BLOCK = 1024
BWD_UNROLL = 1


def nn(a, b):
    return lax.dot_general(a, b, (((1,), (0,)), ((), ())), preferred_element_type=F32)


def nt(a, b):
    return lax.dot_general(a, b, (((1,), (1,)), ((), ())), preferred_element_type=F32)


def tn(a, b):
    return lax.dot_general(a, b, (((0,), (0,)), ((), ())), preferred_element_type=F32)


def hi_lo(value):
    hi = value.astype(BF16)
    return hi, (value - hi.astype(F32)).astype(BF16)


def clip_number(frames, frame):
    one = frames[0]
    two = one + frames[1]
    three = two + frames[2]
    return (
        jnp.where(frame >= one, 1, 0) + jnp.where(frame >= two, 1, 0) + jnp.where(frame >= three, 1, 0)
    )


def frame_facts(frames, res, frame):
    clip = clip_number(frames, frame)
    one = frames[0]
    two = one + frames[1]
    three = two + frames[2]
    start = jnp.where(
        clip == 0, 0, jnp.where(clip == 1, one, jnp.where(clip == 2, two, three))
    )
    height, width = res[3:4, 0:1], res[3:4, 1:2]
    for c in range(CLIPS - 1):
        height = jnp.where(clip == c, res[c : c + 1, 0:1], height)
        width = jnp.where(clip == c, res[c : c + 1, 1:2], width)
    return clip, start, height, width


def column(row):
    return jnp.broadcast_to(row, (8, row.shape[1])).T[:, :1]


def turn_rows(width):
    feat = lax.broadcasted_iota(jnp.int32, (FEAT, width), 0)
    other = lax.broadcasted_iota(jnp.int32, (FEAT, width), 1)
    return jnp.where((feat & 3) * LAT + (feat >> 2) == other, 1.0, 0.0).astype(BF16)


def turn_back():
    feat = lax.broadcasted_iota(jnp.int32, (FEAT, FEAT), 0)
    other = lax.broadcasted_iota(jnp.int32, (FEAT, FEAT), 1)
    return jnp.where((feat & 15) * 4 + (feat >> 4) == other, 1.0, 0.0).astype(BF16)


def cell_order():
    cell = lax.broadcasted_iota(jnp.int32, (CELLS, CELLS), 0)
    place = lax.broadcasted_iota(jnp.int32, (CELLS, CELLS), 1)
    row, col = cell >> 4, cell & 15
    spot = ((row & 1) * 2 + (col & 1)) * 64 + (row >> 1) * PSIDE + (col >> 1)
    return jnp.where(spot == place, 1.0, 0.0).astype(BF16)


def cell_valid(height, width):
    cell = lax.broadcasted_iota(jnp.int32, (1, CELLS), 1)
    return ((cell >> 4) < height) & ((cell & 15) < width)


def stats_kernel(frames, res, enc, place, out):
    slab = lax.axis_index("slab")
    lane = lax.broadcasted_iota(jnp.int32, (FEAT, 128), 1)
    total = jnp.zeros((FEAT, 128), F32)
    for f in range(FRAMES):
        clip, _, height, width = frame_facts(frames, res, slab * FRAMES + f)
        kept = jnp.where(cell_valid(height, width), enc[f].astype(F32), 0.0)
        sums = jnp.sum(kept, axis=1, keepdims=True)
        squares = jnp.sum(kept * kept, axis=1, keepdims=True)
        total = total + jnp.where(lane == clip, sums, 0.0) + jnp.where(lane == clip + 4, squares, 0.0)
    groups = [jnp.sum(total[g * GS : (g + 1) * GS], axis=0, keepdims=True) for g in range(4)]
    payload = jnp.concatenate(groups + [place[...].astype(F32), jnp.zeros((2, 128), F32)], axis=0)
    for j in range(out.shape[0]):
        out[j] = payload


def conv_kernel(frames, res, enc, rim, sums, gain, bias, taps, out, proj):
    totals = jnp.sum(sums[...], axis=0)
    lane = lax.broadcasted_iota(jnp.int32, (8, 128), 1)
    first = lax.axis_index("slab") * FRAMES
    gain_c, bias_c = column(gain[...]), column(bias[...])
    taps_t = taps[...].astype(F32).T.astype(BF16)
    cell = lax.broadcasted_iota(jnp.int32, (1, CELLS), 1)
    row, col = cell >> 4, cell & 15
    for j in range(FRAMES + 2):
        clip, _, height, width = frame_facts(frames, res, jnp.maximum(first - 2 + j, 0))
        count = (frames[clip] * height * width * GS).astype(F32)
        mean = jnp.sum(jnp.where(lane == clip, totals, 0.0), axis=1, keepdims=True) / count
        square = jnp.sum(jnp.where(lane == clip + 4, totals, 0.0), axis=1, keepdims=True) / count
        rstd = lax.rsqrt(square - mean * mean + EPSILON)
        mean_c = jnp.concatenate([jnp.broadcast_to(mean[g : g + 1], (GS, 1)) for g in range(4)], axis=0)
        rstd_c = jnp.concatenate([jnp.broadcast_to(rstd[g : g + 1], (GS, 1)) for g in range(4)], axis=0)
        value = rim[j] if j < 2 else enc[j - 2]
        pre = (value.astype(F32) - mean_c) * rstd_c * gain_c + bias_c
        act = jnp.where(cell_valid(height, width), pre / (1.0 + jnp.exp(-pre)), 0.0)
        proj[j] = nn(taps_t, act.astype(BF16))
    results = []
    for f in range(FRAMES):
        _, start, _, _ = frame_facts(frames, res, first + f)
        source = [jnp.maximum(first + f - 2 + dt, start) - first + 2 for dt in range(3)]
        planes = [proj[source[dt], dt * 144 : (dt + 1) * 144, :] for dt in range(3)]
        joint = planes[0] + planes[1] + planes[2]
        result = jnp.zeros((LAT, CELLS), F32)
        for dx in range(3):
            part = jnp.zeros((LAT, CELLS), F32)
            for dy in range(3):
                tap = (dy * 3 + dx) * LAT
                piece = joint[tap : tap + LAT]
                if dy != 1:
                    piece = pltpu.roll(piece, (-(dy - 1) * SIDE) % CELLS, 1)
                    inside = (row >= 1) if dy == 0 else (row <= SIDE - 2)
                    piece = jnp.where(inside, piece, 0.0)
                part = part + piece
            if dx != 1:
                part = pltpu.roll(part, (-(dx - 1)) % CELLS, 1)
                inside = (col >= 1) if dx == 0 else (col <= SIDE - 2)
                part = jnp.where(inside, part, 0.0)
            result = result + part
        results.append(result.astype(BF16))
    sorted_cells = nn(jnp.concatenate(results, axis=0), cell_order()).astype(BF16)
    for ab in range(4):
        out[ab * LAT : (ab + 1) * LAT, :] = jnp.concatenate(
            [
                sorted_cells[f * LAT : (f + 1) * LAT, ab * 64 : (ab + 1) * 64]
                for f in range(FRAMES)
            ],
            axis=1,
        )


def shift_row(m_hi, m_lo, part):
    unit = jnp.where(lax.broadcasted_iota(jnp.int32, (16, AUG), 1) == FEAT + 1, 1.0, 0.0).astype(BF16)
    return (nt(unit, m_hi[part, :]) + nt(unit, m_lo[part, :]))[0:1]


def share_kernel(pair, one, two, three, out, total):
    value = (pair[...].astype(F32) + two[...].astype(F32)) + (one[...].astype(F32) + three[...].astype(F32))
    total[...] = value
    for j in range(out.shape[0]):
        out[j] = value.astype(BF16)


def cotangent_kernel(grad0, grad1, grad2, grad3, other0, other1, other2, other3, gate, w_out, lat_sorted, d_attn, d_out, latents):
    place = lax.axis_index("mp")
    core, level = lax.rem(place, 2), lax.div(place, 2)
    total = jnp.zeros((ROWS, HEADS * HD), F32)
    for k, grads in enumerate(((grad0, other0), (grad1, other1), (grad2, other2), (grad3, other3))):
        for side in range(2):
            m = lax.rem(level - k + 4, 4) * 2 + (core if side == 0 else 1 - core)
            cols = pl.ds(pl.multiple_of(m * 384, 128), 384)
            part = (grads[side][...].astype(F32) * gate[:, cols]).astype(BF16)
            d_attn[m] = part
            total = total + nt(part, w_out[:, cols])
    d_out[...] = total.astype(BF16)
    by_frame = jnp.concatenate(
        [
            jnp.concatenate(
                [lat_sorted[ab * LAT : (ab + 1) * LAT, f * 64 : (f + 1) * 64] for ab in range(4)], axis=1
            )
            for f in range(FRAMES)
        ],
        axis=0,
    )
    hi, lo = hi_lo(by_frame)
    order = cell_order()
    values = nt(hi, order) + nt(lo, order)
    for f in range(FRAMES):
        latents[f] = values[f * LAT : (f + 1) * LAT]


def prepare_kernel(
    embed_w,
    embed_b,
    shift,
    scale,
    w_hbm,
    gram_hi,
    gram_lo,
    m_hi,
    m_lo,
    m_k,
    centered_two,
    own_rows,
    window,
    w_qkv,
    arrived,
):
    fetch = pltpu.make_async_copy(w_hbm, w_qkv, arrived)
    fetch.start()
    row = lax.broadcasted_iota(jnp.int32, (16, D), 0)
    extra = jnp.where(row == 0, embed_b[...], 0.0)
    augmented = jnp.concatenate([nn(turn_back(), embed_w[...]), extra], axis=0)
    centered = augmented - jnp.mean(augmented, axis=1, keepdims=True)
    c_hi, c_lo = hi_lo(centered)
    centered_two[:AUG, :] = c_hi
    centered_two[AUG:, :] = c_lo
    gram = (nt(c_hi, c_hi) + nt(c_hi, c_lo) + nt(c_lo, c_hi)) * (1.0 / D)
    g_hi, g_lo = hi_lo(gram)
    gram_hi[...] = g_hi
    gram_lo[...] = g_lo
    row = lax.broadcasted_iota(jnp.int32, (AUG, D), 0)
    modulated = jnp.where(row == FEAT + 1, shift[...], centered * (1.0 + scale[...]))
    a_hi, a_lo = hi_lo(modulated)
    fetch.wait()
    both = nn(jnp.concatenate([a_hi, a_lo], axis=0), w_qkv[...])
    turned = (both[:AUG] + both[AUG:]).T
    t_hi, t_lo = hi_lo(turned)
    m_hi[...] = t_hi
    m_lo[...] = t_lo
    for h in range(HEADS):
        keys = slice(h * 384 + 128, h * 384 + 256)
        m_k[h * HD : (h + 1) * HD, :] = jnp.concatenate([t_hi[keys], t_hi[keys], t_lo[keys]], axis=1)
    window[...] = modulated.T
    slab = lax.axis_index("slab")
    o_hi, o_lo = hi_lo(window[pl.ds(pl.multiple_of(slab * 192, 64), 192), :])
    own_rows[...] = jnp.concatenate([o_hi, o_lo], axis=1)


def forward_kernel(
    frames,
    res,
    patches,
    place,
    gram_hi,
    gram_lo,
    m_k,
    m_hi,
    m_lo,
    d_out,
    q_gain,
    k_gain,
    grad_out,
    w_out,
    d_attn,
    embed_w,
    embed_b,
    attn_mine,
    attn_other,
    g_part0,
    g_part1,
    g_part2,
    g_part3,
    hidden_cols,
    early,
    g_own,
    s_sent,
    k_sent,
    rk_t,
    q_ext,
    q_norm,
    q_facts,
    u_cat,
    s_own,
):
    s_t, k_t = s_sent.buffer, k_sent.buffer
    blocks = patches.shape[0]
    row_aug = lax.broadcasted_iota(jnp.int32, (AUG, ROWS), 0)
    row16 = lax.broadcasted_iota(jnp.int32, (16, ROWS), 0)
    token = lax.broadcasted_iota(jnp.int32, (1, ROWS), 1)
    position = lax.broadcasted_iota(jnp.int32, (ROWS, ROWS), 0).astype(F32)
    base = (lax.axis_index("slab") * ROWS).astype(F32)
    k_gain_c = column(k_gain[...])
    one_row = jnp.where(row16 == 0, 1.0, 0.0).astype(BF16)

    def prepare(j, carry):
        x_q, clip_q = carry
        block = pl.ds(pl.multiple_of(j * ROWS, ROWS), ROWS)
        x_aug = jnp.concatenate([patches[j], one_row], axis=0)
        x_f = x_aug.astype(F32)
        gx = nn(gram_hi[...], x_aug) + nn(gram_lo[...], x_aug)
        rstd = lax.rsqrt(jnp.sum(gx * x_f, axis=0, keepdims=True) + EPSILON)
        s_hi, s_lo = hi_lo(jnp.where(row_aug == FEAT + 1, 1.0, x_f * rstd))
        s_t[:AUG, block] = s_hi
        s_t[AUG:, block] = s_lo
        clip = clip_number(frames, j * FRAMES + (token >> 6))
        height = jnp.zeros((1, ROWS), jnp.int32)
        width = jnp.zeros((1, ROWS), jnp.int32)
        for c in range(CLIPS):
            height = jnp.where(clip == c, res[c : c + 1, 0:1], height)
            width = jnp.where(clip == c, res[c : c + 1, 1:2], width)
        valid = (2 * ((token >> 3) & 7) < height) & (2 * (token & 7) < width)
        member = row16 == clip
        mask = jnp.where((row16 < CLIPS) & ~(member & valid), OFF, 0.0).astype(BF16)
        both = nn(m_k[...], jnp.concatenate([s_hi, s_lo, s_hi], axis=0))
        for h in range(HEADS):
            k = both[h * HD : (h + 1) * HD]
            rk = lax.rsqrt(jnp.mean(k * k, axis=0, keepdims=True) + EPSILON)
            rk_t[h, :, block] = jnp.broadcast_to(rk, (8, ROWS))
            k_t[h, :HD, block] = (k * rk * k_gain_c).astype(BF16)
            k_t[h, HD:, block] = mask
        spot = jnp.concatenate([place[j, 4:5, :], place[j, 5:6, :]], axis=1)
        chosen = jnp.where(spot == position + base, 1.0, 0.0).astype(BF16)
        x_q = x_q + nt(chosen, x_aug)
        clip_q = clip_q + nt(chosen, jnp.where(member, 1.0, 0.0).astype(BF16))
        return x_q, clip_q

    x_q, clip_q = lax.fori_loop(
        0, blocks, prepare, (jnp.zeros((ROWS, AUG), F32), jnp.zeros((ROWS, 16), F32)), unroll=PREPARE_UNROLL
    )
    s_sent.send()
    k_sent.send()
    x_qb = x_q.astype(BF16)
    own_cols = pl.ds(pl.multiple_of(lax.axis_index("mp") * 384, 128), 384)
    embed_cols = nn(turn_back(), embed_w.ready()[:, own_cols]).astype(BF16)
    hidden_cols[...] = (nn(x_qb[:, :FEAT], embed_cols) + embed_b[:, own_cols]).astype(BF16)
    g_own[...] = nn(turn_rows(AUG), tn(x_qb, grad_out.ready()[...]).astype(BF16))
    gx_q = nn(x_qb, gram_hi[...]) + nn(x_qb, gram_lo[...])
    rstd_q = lax.rsqrt(jnp.sum(gx_q * x_q, axis=1, keepdims=True) + EPSILON)
    lane_aug = lax.broadcasted_iota(jnp.int32, (ROWS, AUG), 1)
    s_q = jnp.where(lane_aug == FEAT + 1, 1.0, x_q * rstd_q)
    s_own[...] = s_q
    s_qhi, s_qlo = hi_lo(s_q)
    clip_qb = clip_q.astype(BF16)
    lane = lax.broadcasted_iota(jnp.int32, (ROWS, 128), 1)
    facts = jnp.zeros((ROWS, 128), F32)
    for h in range(HEADS):
        mine = slice(h * 384, h * 384 + 128)
        q = nt(s_qhi, m_hi[mine, :]) + nt(s_qlo, m_hi[mine, :]) + nt(s_qhi, m_lo[mine, :])
        rq = lax.rsqrt(jnp.mean(q * q, axis=1, keepdims=True) + EPSILON)
        qn = q * rq
        q_norm[h] = qn
        q_ext[h, :, :HD] = (qn * (q_gain[...] * (HD**-0.5 * LOG2E))).astype(BF16)
        q_ext[h, :, HD:] = clip_qb
        facts = jnp.where(lane == h, rq, facts)

    def forward(j, totals):
        block = pl.ds(pl.multiple_of(j * FWD_BLOCK, FWD_BLOCK), FWD_BLOCK)
        s_block = s_t[:, block]
        probs = [jnp.exp2(nn(q_ext[h], k_t[h, :, block])).astype(BF16) for h in range(HEADS)]
        return tuple(totals[h] + nt(probs[h], s_block) for h in range(HEADS))

    totals = lax.fori_loop(
        0, 4096 // FWD_BLOCK, forward, (jnp.zeros((ROWS, 2 * AUG), F32),) * HEADS, unroll=FWD_UNROLL
    )
    heads = []
    d_out = d_out.ready()
    for h in range(HEADS):
        inv_l = 1.0 / totals[h][:, FEAT + 1 : FEAT + 2]
        z_hi, z_lo = hi_lo((totals[h][:, :AUG] + totals[h][:, AUG:]) * inv_l)
        mine = slice(h * 384 + 256, h * 384 + 384)
        att = (nt(z_hi, m_hi[mine, :]) + nt(z_lo, m_hi[mine, :]) + nt(z_hi, m_lo[mine, :])).astype(BF16)
        heads.append(att)
        d_bf = d_out[:, h * HD : (h + 1) * HD]
        early[:, h * HD : (h + 1) * HD] = tn(z_hi, d_bf)
        do = d_bf.astype(F32)
        shift_v = shift_row(m_hi, m_lo, mine)
        weight = jnp.sum(do * (att.astype(F32) - shift_v), axis=1, keepdims=True) * inv_l
        facts = jnp.where(lane == 2 + h, weight, facts)
        u = (nn(d_bf, m_hi[mine, :]) + nn(d_bf, m_lo[mine, :])) * inv_l
        u_hi, u_lo = hi_lo(jnp.where(lane_aug == FEAT + 1, 0.0, u))
        u_cat[h] = jnp.concatenate([u_hi, u_lo, u_hi], axis=1)
    q_facts[...] = facts
    att_all = jnp.concatenate(heads, axis=1)
    place_mp, slab = lax.axis_index("mp"), lax.axis_index("slab")
    core, level = lax.rem(place_mp, 2), lax.div(place_mp, 2)
    y_pos, x_pos = lax.div(slab, 4), lax.rem(slab, 4)
    d_attn, w_out = d_attn.ready(), w_out.ready()
    for k, g_part in enumerate((g_part0, g_part1, g_part2, g_part3)):
        y_to = lax.rem(y_pos + k, 4)
        for half in range(2):
            both = tn(d_attn[2 * y_to + half], att_all).astype(BF16)
            for side in range(2):
                slot = lax.rem(2 * half + side - x_pos + 4, 4)
                g_part.buffer[slot] = both[side * 192 : (side + 1) * 192]
        g_part.send()
    for side, attn_part in enumerate((attn_other, attn_mine)):
        for k in range(4):
            m = 2 * lax.rem(level + k, 4) + (core if side == 1 else 1 - core)
            cols = pl.ds(pl.multiple_of(m * 384, 128), 384)
            attn_part.buffer[k] = nn(att_all, w_out[:, cols]).astype(BF16)
        attn_part.send()


def backward_kernel(
    s_hbm,
    k_hbm,
    rk_t,
    q_ext,
    q_norm,
    q_facts,
    u_cat,
    s_own,
    m_hi,
    m_lo,
    q_gain,
    k_gain,
    early,
    mod_scale,
    centered,
    w_hbm,
    sums,
    y_mine,
    y_other,
    q_t,
    w_qkv,
    arrived,
    s_t,
    k_t,
    s_sems,
    k_sems,
):
    def fetch_block(j):
        block = pl.ds(pl.multiple_of(j * BWD_BLOCK, BWD_BLOCK), BWD_BLOCK)
        return (
            pltpu.make_async_copy(s_hbm.at[:, block], s_t.at[:, block], s_sems.at[j]),
            pltpu.make_async_copy(k_hbm.at[:, :, block], k_t.at[:, :, block], k_sems.at[j]),
        )

    for j in range(4096 // BWD_BLOCK):
        for copy in fetch_block(j):
            copy.start()
    fetch = pltpu.make_async_copy(w_hbm, w_qkv, arrived)
    fetch.start()
    shift_k = []
    for h in range(HEADS):
        q_t[h] = q_ext[h, :, :HD].astype(F32).T.astype(BF16)
        mine = slice(h * 384 + 128, h * 384 + 256)
        shift_k.append(
            m_hi[mine, FEAT + 1 : FEAT + 2].astype(F32) + m_lo[mine, FEAT + 1 : FEAT + 2].astype(F32)
        )
    k_gain_c = column(k_gain[...])
    gain_back = k_gain_c * (1.0 / LOG2E)
    gain_inv = 1.0 / k_gain_c
    weights = [q_facts[:, 2 + h : 3 + h] for h in range(HEADS)]

    def backward(j, carry):
        grad_qs, p_k, quad = carry
        for copy in fetch_block(j):
            copy.wait()
        block = pl.ds(pl.multiple_of(j * BWD_BLOCK, BWD_BLOCK), BWD_BLOCK)
        s_hi = s_t[:AUG, block]
        s_cat = jnp.concatenate([s_hi, s_hi, s_t[AUG:, block]], axis=0)
        m2 = jnp.zeros((1, BWD_BLOCK), F32)
        new_q, dks = [], []
        for h in range(HEADS):
            keys = k_t[h, :HD, block]
            p = jnp.exp2(nn(q_ext[h], k_t[h, :, block]))
            raw = p * nn(u_cat[h], s_cat)
            m2 = m2 + jnp.sum(raw, axis=0, keepdims=True)
            d_score = (raw - p * weights[h]).astype(BF16)
            new_q.append(grad_qs[h] + nt(d_score, keys))
            scaled = nn(q_t[h], d_score) * gain_back
            kn = keys.astype(F32) * gain_inv
            rk = rk_t[h, 0:1, block]
            dk = rk * (scaled - kn * jnp.mean(scaled * kn, axis=0, keepdims=True))
            m2 = m2 + jnp.sum(dk * (kn * (1.0 / rk) - shift_k[h]), axis=0, keepdims=True)
            dks.append(dk.astype(BF16))
        p_k = p_k + nt(s_hi, jnp.concatenate(dks, axis=0))
        quad = quad + nt((s_hi.astype(F32) * m2).astype(BF16), s_hi)
        return tuple(new_q), p_k, quad

    grad_qs, p_k, quad = lax.fori_loop(
        0,
        4096 // BWD_BLOCK,
        backward,
        (
            (jnp.zeros((ROWS, HD), F32),) * HEADS,
            jnp.zeros((AUG, HEADS * HD), F32),
            jnp.zeros((AUG, AUG), F32),
        ),
        unroll=BWD_UNROLL,
    )
    s_q = s_own[...]
    s_qhi = s_q.astype(BF16)
    m2_q = jnp.zeros((ROWS, 1), F32)
    pieces = []
    for h in range(HEADS):
        mine = slice(h * 384, h * 384 + 128)
        rq = q_facts[:, h : h + 1]
        qn = q_norm[h]
        scaled = grad_qs[h] * (q_gain[...] * HD**-0.5)
        dq = rq * (scaled - qn * jnp.mean(scaled * qn, axis=1, keepdims=True))
        shift_q = shift_row(m_hi, m_lo, mine)
        m2_q = m2_q + jnp.sum(dq * (qn * (1.0 / rq) - shift_q), axis=1, keepdims=True)
        pieces += [tn(s_qhi, dq.astype(BF16)), p_k[:, h * HD : (h + 1) * HD], early[:, h * HD : (h + 1) * HD]]
    p_all = jnp.concatenate(pieces, axis=1).astype(BF16)
    sums[...] = p_all
    quad = ((quad + tn((s_q * m2_q).astype(BF16), s_qhi)) * (1.0 / D)).astype(BF16)
    turn = turn_rows(AUG)
    turned = nn(turn, p_all).astype(BF16)
    quad = nn(turn, quad).astype(BF16)
    fetch.wait()
    back = nt(turned, w_qkv[...]) * (1.0 + mod_scale[...])
    back = back - jnp.mean(back, axis=1, keepdims=True)
    back = (back - nn(jnp.concatenate([quad, quad], axis=1), centered[...])).astype(BF16)
    place = lax.axis_index("mp")
    core, level = lax.rem(place, 2), lax.div(place, 2)
    for z in range(4):
        slot = lax.rem(z - level + 4, 4)
        even = back[:, 2 * z * 384 : (2 * z + 1) * 384]
        odd = back[:, (2 * z + 1) * 384 : (2 * z + 2) * 384]
        y_mine[slot] = jnp.where(core == 0, even, odd)
        y_other[slot] = jnp.where(core == 0, odd, even)


def weights_kernel(own, one, two, three, own_rows, g_qkv, g_embed):
    total = (own[...].astype(F32) + two[...].astype(F32)) + (one[...].astype(F32) + three[...].astype(F32))
    p_all = total[:, :768].astype(BF16)
    g_qkv[...] = nn(own_rows[...], jnp.concatenate([p_all, p_all], axis=0))
    g_embed[...] = total[:FEAT, 768:]


VMEM = pl.BlockSpec(memory_space=pltpu.VMEM)
SMEM = pl.BlockSpec(memory_space=pltpu.SMEM)
ANY = pl.BlockSpec(memory_space=pl.ANY)


class Fetched:
    def __init__(self, source, buffer, sem):
        self.buffer, self.copy = buffer, pltpu.make_async_copy(source, buffer, sem)
        self.copy.start()

    def ready(self):
        self.copy.wait()
        return self.buffer


class Sent:
    def __init__(self, target, buffer, sem):
        self.buffer, self.copy = buffer, pltpu.make_async_copy(buffer, target, sem)

    def send(self):
        self.copy.start()


def call(kernel, inputs, outputs, scratch, flops, mib, places, out_places=None):
    single = not isinstance(outputs, tuple)
    outs = (outputs,) if single else outputs
    out_places = out_places or "v" * len(outs)
    staged = [
        (i, pltpu.VMEM(v.shape, v.dtype)) for i, (p, v) in enumerate(zip(places, inputs, strict=True)) if p == "l"
    ]
    sent = [(i, pltpu.VMEM(o.shape, o.dtype)) for i, (p, o) in enumerate(zip(out_places, outs, strict=True)) if p == "e"]
    n_in, n_out, n_stage, n_sent = len(inputs), len(outs), len(staged), len(sent)

    def wrapped(*refs):
        ins, results = list(refs[:n_in]), list(refs[n_in : n_in + n_out])
        rest = refs[n_in + n_out :]
        buffers, rest = rest[:n_stage], rest[n_stage:]
        holds, rest = rest[:n_sent], rest[n_sent:]
        sems, rest = rest[: n_stage + n_sent], rest[n_stage + n_sent :]
        for slot, (i, _) in enumerate(staged):
            ins[i] = Fetched(ins[i], buffers[slot], sems[slot])
        for slot, (i, _) in enumerate(sent):
            results[i] = Sent(results[i], holds[slot], sems[n_stage + slot])
        kernel(*ins, *results, *rest)
        for i, _ in sent:
            results[i].copy.wait()

    specs = {"v": VMEM, "e": ANY, "l": ANY, "r": ANY, "s": SMEM}
    result = pl.pallas_call(
        wrapped,
        out_shape=outs,
        in_specs=[specs[p] for p in places],
        out_specs=tuple(specs[p] for p in out_places),
        scratch_shapes=[b for _, b in staged]
        + [b for _, b in sent]
        + [pltpu.SemaphoreType.DMA] * (n_stage + n_sent)
        + scratch,
        compiler_params=pltpu.CompilerParams(vmem_limit_bytes=mib * MIB),
        cost_estimate=pl.CostEstimate(flops=flops, bytes_accessed=1 << 20, transcendentals=0),
    )(*inputs)
    return result[0] if single else result


def shift_by(value, axis, move):
    return lax.ppermute(value, axis, [(i, move(i)) for i in range(lax.axis_size(axis))])


def along_x(k):
    return lambda i: (i // 4) * 4 + (i % 4 + k) % 4


def along_y(k):
    return lambda i: ((i // 4 + k) % 4) * 4 + i % 4


def along_z(k):
    return lambda i: ((i // 2 + k) % 4) * 2 + i % 2


def sum_of_four(value, axis, move, kind):
    sent = value.astype(kind)
    one, two, three = (shift_by(sent, axis, move(k)).astype(F32) for k in (1, 2, 3))
    return (sent.astype(F32) + two) + (one + three)


def level_sum(pair):
    one, two, three = (shift_by(pair[k], "mp", along_z(k)).astype(F32) for k in (1, 2, 3))
    return (pair[0].astype(F32) + two) + (one + three)


def body(
    enc_feat,
    gn_gain,
    gn_bias,
    conv_w,
    clip_frames,
    clip_res,
    token_place,
    embed_w,
    embed_b,
    mod_shift,
    mod_scale,
    mod_gate,
    w_qkv,
    q_gain,
    k_gain,
    w_out,
    grad_out,
):
    slabs = lax.axis_size("slab")
    mp_size = lax.axis_size("mp")
    mp_pos = lax.axis_index("mp")
    cols_dev = D // mp_size
    row_cols = D // slabs

    clip_res = jnp.pad(clip_res, ((0, 4), (0, 126)))
    all_sent = call(
        stats_kernel,
        (clip_frames, clip_res, enc_feat, token_place.reshape(2, 128)),
        jax.ShapeDtypeStruct((slabs, 8, 128), F32),
        [],
        1 << 20,
        60,
        "svvv",
    )
    all_stats = lax.all_to_all(all_sent, "slab", split_axis=0, concat_axis=0, tiled=True)
    rim = shift_by(enc_feat[FRAMES - 2 :], "slab", lambda i: (i + 1) % slabs)
    rim, grad_sent = lax.optimization_barrier((rim, grad_out))
    grads = (grad_sent,) + tuple(shift_by(grad_sent, "mp", along_z(k)) for k in (1, 2, 3))
    embed_late, _ = lax.optimization_barrier((embed_b, all_sent))
    gram_hi, gram_lo, m_hi, m_lo, m_k, centered, own_rows = call(
        prepare_kernel,
        (embed_w, embed_late[None, :], mod_shift[None, :], mod_scale[None, :], w_qkv),
        (
            jax.ShapeDtypeStruct((AUG, AUG), BF16),
            jax.ShapeDtypeStruct((AUG, AUG), BF16),
            jax.ShapeDtypeStruct((768, AUG), BF16),
            jax.ShapeDtypeStruct((768, AUG), BF16),
            jax.ShapeDtypeStruct((HEADS * HD, 3 * AUG), BF16),
            jax.ShapeDtypeStruct((2 * AUG, D), BF16),
            jax.ShapeDtypeStruct((row_cols, 2 * AUG), BF16),
        ),
        [pltpu.VMEM((D, AUG), F32), pltpu.VMEM((D, 768), BF16), pltpu.SemaphoreType.DMA],
        1 << 33,
        60,
        "vvvvr",
    )
    gain, gram_hi = lax.optimization_barrier((gn_gain, gram_hi))
    partial = call(
        conv_kernel,
        (clip_frames, clip_res, enc_feat, rim, all_stats, gain[None, :], gn_bias[None, :], conv_w),
        jax.ShapeDtypeStruct((FEAT, CELLS), BF16),
        [pltpu.VMEM((FRAMES + 2, 432, CELLS), F32)],
        1 << 28,
        60,
        "svvvvvvv",
    )
    partial, grads = lax.optimization_barrier((partial, grads))
    pair = (partial.astype(F32) + shift_by(partial, "mp", lambda i: i ^ 1).astype(F32)).astype(BF16)
    patches_sent, lat_sorted = call(
        share_kernel,
        (pair,) + tuple(shift_by(pair, "mp", along_z(k)) for k in (1, 2, 3)),
        (
            jax.ShapeDtypeStruct((slabs, FEAT, CELLS), BF16),
            jax.ShapeDtypeStruct((FEAT, CELLS), F32),
        ),
        [],
        1 << 20,
        4,
        "vvvv",
    )
    all_patches = lax.all_to_all(patches_sent, "slab", split_axis=0, concat_axis=0, tiled=True)

    grads, lat_sorted = lax.optimization_barrier((grads, lat_sorted))
    others = tuple(shift_by(block, "mp", lambda i: i ^ 1) for block in grads)
    d_attn, d_out, latents = call(
        cotangent_kernel,
        (*grads, *others, mod_gate[None, :], w_out, lat_sorted),
        (
            jax.ShapeDtypeStruct((mp_size, ROWS, cols_dev), BF16),
            jax.ShapeDtypeStruct((ROWS, HEADS * HD), BF16),
            jax.ShapeDtypeStruct((FRAMES, LAT, CELLS), F32),
        ),
        [],
        1 << 32,
        60,
        "vvvvvvvvvvv",
    )

    (
        attn_mine,
        attn_other,
        *g_parts,
        hidden_cols,
        early,
        g_own,
        s_t,
        k_t,
        rk_t,
        q_ext,
        q_norm,
        q_facts,
        u_cat,
        s_own,
    ) = call(
        forward_kernel,
        (
            clip_frames,
            clip_res,
            all_patches,
            all_stats,
            gram_hi,
            gram_lo,
            m_k,
            m_hi,
            m_lo,
            d_out,
            q_gain[None, :],
            k_gain[None, :],
            grad_out,
            w_out,
            d_attn,
            embed_w,
            embed_b[None, :],
        ),
        (
            *(jax.ShapeDtypeStruct((4, ROWS, cols_dev), BF16),) * 2,
            *(jax.ShapeDtypeStruct((4, row_cols, HEADS * HD), BF16),) * 4,
            jax.ShapeDtypeStruct((ROWS, cols_dev), BF16),
            jax.ShapeDtypeStruct((AUG, 256), F32),
            jax.ShapeDtypeStruct((FEAT, cols_dev), F32),
            jax.ShapeDtypeStruct((2 * AUG, 4096), BF16),
            jax.ShapeDtypeStruct((HEADS, EXT, 4096), BF16),
            jax.ShapeDtypeStruct((HEADS, 8, 4096), F32),
            jax.ShapeDtypeStruct((HEADS, ROWS, EXT), BF16),
            jax.ShapeDtypeStruct((HEADS, ROWS, HD), F32),
            jax.ShapeDtypeStruct((ROWS, 128), F32),
            jax.ShapeDtypeStruct((HEADS, ROWS, 3 * AUG), BF16),
            jax.ShapeDtypeStruct((ROWS, AUG), F32),
        ),
        [],
        1 << 33,
        60,
        "svvvvvvvvlvvllllv",
        "eeeeeevvveevvvvvv",
    )
    attn_got = shift_by(attn_other, "mp", lambda i: i ^ 1)
    g_one = shift_by(g_parts[1], "slab", along_y(1))
    g_three = shift_by(g_parts[3], "slab", along_y(3))
    sums, y_mine, y_other = call(
        backward_kernel,
        (
            s_t,
            k_t,
            rk_t,
            q_ext,
            q_norm,
            q_facts,
            u_cat,
            s_own,
            m_hi,
            m_lo,
            q_gain[None, :],
            k_gain[None, :],
            early,
            mod_scale[None, :],
            centered,
            w_qkv,
        ),
        (
            jax.ShapeDtypeStruct((AUG, 768), BF16),
            jax.ShapeDtypeStruct((4, FEAT, cols_dev), BF16),
            jax.ShapeDtypeStruct((4, FEAT, cols_dev), BF16),
        ),
        [
            pltpu.VMEM((HEADS, HD, ROWS), BF16),
            pltpu.VMEM((D, 768), BF16),
            pltpu.SemaphoreType.DMA,
            pltpu.VMEM((2 * AUG, 4096), BF16),
            pltpu.VMEM((HEADS, EXT, 4096), BF16),
            pltpu.SemaphoreType.DMA((4096 // BWD_BLOCK,)),
            pltpu.SemaphoreType.DMA((4096 // BWD_BLOCK,)),
        ],
        1 << 34,
        60,
        "rrvvvvvvvvvvvvvr",
    )

    sums, y_mine, y_other, g_one, g_three, attn_got = lax.optimization_barrier(
        (sums, y_mine, y_other, g_one, g_three, attn_got)
    )
    y_got = shift_by(y_other, "mp", lambda i: i ^ 1)
    y_pair = (y_mine.astype(F32) + y_got.astype(F32)).astype(BF16)
    g_two = shift_by(g_parts[2], "slab", along_y(2))
    embed_part = level_sum(y_pair) + g_own
    payload = jnp.concatenate([sums, jnp.pad(embed_part, ((0, AUG - FEAT), (0, 0))).astype(BF16)], axis=1)
    payload, attn_mine = lax.optimization_barrier((payload, attn_mine))
    sent = tuple(shift_by(payload, "slab", along_x(k)) for k in (1, 2, 3))
    total = (
        (payload.astype(F32) + sent[1].astype(F32)) + (sent[0].astype(F32) + sent[2].astype(F32))
    ).astype(BF16)
    attn_pair = (attn_mine.astype(F32) + attn_got.astype(F32)).astype(BF16)
    attn_cols = level_sum(attn_pair)
    gate_cols = lax.dynamic_slice_in_dim(mod_gate, mp_pos * cols_dev, cols_dev, 0)
    block_out = (hidden_cols.astype(F32) + gate_cols * attn_cols).astype(BF16)
    received = tuple(shift_by(total, "slab", along_y(k)) for k in (1, 2, 3))
    total, g_two = lax.optimization_barrier((total, g_two))
    g_sum = (
        (g_parts[0].astype(F32) + g_two.astype(F32)) + (g_one.astype(F32) + g_three.astype(F32))
    ).astype(BF16)
    g_out = g_sum[0].astype(F32)
    for k in (1, 2, 3):
        g_out = g_out + shift_by(g_sum[k], "slab", along_x(k)).astype(F32)
    g_out = g_out.T
    g_qkv, g_embed = call(
        weights_kernel,
        (total, *received, own_rows),
        (
            jax.ShapeDtypeStruct((row_cols, 768), F32),
            jax.ShapeDtypeStruct((FEAT, cols_dev), F32),
        ),
        [],
        1 << 26,
        4,
        "vvvvv",
    )
    return (latents, block_out, g_qkv, g_out, g_embed)


def solution(mesh):
    in_specs = (
        P(("dp", "slab"), "mp", None),
        P("mp"),
        P("mp"),
        P("mp", None),
        P("dp"),
        P("dp", None),
        P(("dp", "slab")),
        P(),
        P(),
        P("dp"),
        P("dp"),
        P("dp"),
        P(None, "mp"),
        P(),
        P(),
        P("mp", None),
        P(("dp", "slab"), "mp"),
    )
    out_specs = (
        P(("dp", "slab"), None, None),
        P(("dp", "slab"), "mp"),
        P(("dp", "slab"), "mp"),
        P(("dp", "mp"), "slab"),
        P("dp", "mp"),
    )
    return jax.shard_map(body, mesh=mesh, in_specs=in_specs, out_specs=out_specs, check_vma=False)
```

```python
import functools

import jax
import jax.numpy as jnp
from jax import lax
from jax.experimental import pallas as pl
from jax.experimental.pallas import tpu as pltpu
from jax.sharding import PartitionSpec as P

D = 3072
HD = 128
LAT = 16
CLIPS = 4
SIDE = 16
PSIDE = 8
CELLS = 256
GS = 16
HEADS = 2
ROWS = 256
FRAMES = 4
FEAT = 64
AUG = 80
EXT = 144
EPSILON = 1e-06
HIGHEST = lax.Precision.HIGHEST
LOG2E = 1.4426950408889634
OFF = -1e30
F32 = jnp.float32
BF16 = jnp.bfloat16
MIB = 1024 * 1024
PREPARE_UNROLL = 4
FWD_BLOCK = 1024
FWD_UNROLL = 1
BWD_BLOCK = 1024
BWD_UNROLL = 1


def nn(a, b):
    return lax.dot_general(a, b, (((1,), (0,)), ((), ())), preferred_element_type=F32)


def nt(a, b):
    return lax.dot_general(a, b, (((1,), (1,)), ((), ())), preferred_element_type=F32)


def tn(a, b):
    return lax.dot_general(a, b, (((0,), (0,)), ((), ())), preferred_element_type=F32)


def hi_lo(value):
    hi = value.astype(BF16)
    return hi, (value - hi.astype(F32)).astype(BF16)


def clip_number(frames, frame):
    one = frames[0]
    two = one + frames[1]
    three = two + frames[2]
    return (
        jnp.where(frame >= one, 1, 0) + jnp.where(frame >= two, 1, 0) + jnp.where(frame >= three, 1, 0)
    )


def frame_facts(frames, res, frame):
    clip = clip_number(frames, frame)
    one = frames[0]
    two = one + frames[1]
    three = two + frames[2]
    start = jnp.where(
        clip == 0, 0, jnp.where(clip == 1, one, jnp.where(clip == 2, two, three))
    )
    height, width = res[3:4, 0:1], res[3:4, 1:2]
    for c in range(CLIPS - 1):
        height = jnp.where(clip == c, res[c : c + 1, 0:1], height)
        width = jnp.where(clip == c, res[c : c + 1, 1:2], width)
    return clip, start, height, width


def column(row):
    return jnp.broadcast_to(row, (8, row.shape[1])).T[:, :1]


def turn_rows(width):
    feat = lax.broadcasted_iota(jnp.int32, (FEAT, width), 0)
    other = lax.broadcasted_iota(jnp.int32, (FEAT, width), 1)
    return jnp.where((feat & 3) * LAT + (feat >> 2) == other, 1.0, 0.0).astype(BF16)


def turn_back():
    feat = lax.broadcasted_iota(jnp.int32, (FEAT, FEAT), 0)
    other = lax.broadcasted_iota(jnp.int32, (FEAT, FEAT), 1)
    return jnp.where((feat & 15) * 4 + (feat >> 4) == other, 1.0, 0.0).astype(BF16)


def cell_order():
    cell = lax.broadcasted_iota(jnp.int32, (CELLS, CELLS), 0)
    place = lax.broadcasted_iota(jnp.int32, (CELLS, CELLS), 1)
    row, col = cell >> 4, cell & 15
    spot = ((row & 1) * 2 + (col & 1)) * 64 + (row >> 1) * PSIDE + (col >> 1)
    return jnp.where(spot == place, 1.0, 0.0).astype(BF16)


def cell_valid(height, width):
    cell = lax.broadcasted_iota(jnp.int32, (1, CELLS), 1)
    return ((cell >> 4) < height) & ((cell & 15) < width)


def stats_kernel(frames, res, enc, place, out):
    slab = lax.axis_index("slab")
    lane = lax.broadcasted_iota(jnp.int32, (FEAT, 128), 1)
    total = jnp.zeros((FEAT, 128), F32)
    for f in range(FRAMES):
        clip, _, height, width = frame_facts(frames, res, slab * FRAMES + f)
        kept = jnp.where(cell_valid(height, width), enc[f].astype(F32), 0.0)
        sums = jnp.sum(kept, axis=1, keepdims=True)
        squares = jnp.sum(kept * kept, axis=1, keepdims=True)
        total = total + jnp.where(lane == clip, sums, 0.0) + jnp.where(lane == clip + 4, squares, 0.0)
    groups = [jnp.sum(total[g * GS : (g + 1) * GS], axis=0, keepdims=True) for g in range(4)]
    payload = jnp.concatenate(groups + [place[...].astype(F32), jnp.zeros((2, 128), F32)], axis=0)
    for j in range(out.shape[0]):
        out[j] = payload


def taps_kernel(taps, out):
    out[...] = taps[...].astype(F32).T.astype(BF16)


def conv_kernel(frames, res, enc, rim, sums, gain, bias, taps, out, proj):
    totals = jnp.sum(sums[...], axis=0)
    lane = lax.broadcasted_iota(jnp.int32, (8, 128), 1)
    first = lax.axis_index("slab") * FRAMES
    gain_c, bias_c = column(gain[...]), column(bias[...])
    cell = lax.broadcasted_iota(jnp.int32, (1, CELLS), 1)
    row, col = cell >> 4, cell & 15
    for j in range(FRAMES + 2):
        clip, _, height, width = frame_facts(frames, res, jnp.maximum(first - 2 + j, 0))
        count = (frames[clip] * height * width * GS).astype(F32)
        mean = jnp.sum(jnp.where(lane == clip, totals, 0.0), axis=1, keepdims=True) / count
        square = jnp.sum(jnp.where(lane == clip + 4, totals, 0.0), axis=1, keepdims=True) / count
        rstd = lax.rsqrt(square - mean * mean + EPSILON)
        mean_c = jnp.concatenate([jnp.broadcast_to(mean[g : g + 1], (GS, 1)) for g in range(4)], axis=0)
        rstd_c = jnp.concatenate([jnp.broadcast_to(rstd[g : g + 1], (GS, 1)) for g in range(4)], axis=0)
        value = rim[j] if j < 2 else enc[j - 2]
        pre = (value.astype(F32) - mean_c) * rstd_c * gain_c + bias_c
        act = jnp.where(cell_valid(height, width), pre / (1.0 + jnp.exp(-pre)), 0.0)
        proj[j] = nn(taps[...], act.astype(BF16))
    results = []
    for f in range(FRAMES):
        _, start, _, _ = frame_facts(frames, res, first + f)
        source = [jnp.maximum(first + f - 2 + dt, start) - first + 2 for dt in range(3)]
        planes = [proj[source[dt], dt * 144 : (dt + 1) * 144, :] for dt in range(3)]
        joint = planes[0] + planes[1] + planes[2]
        result = jnp.zeros((LAT, CELLS), F32)
        for dx in range(3):
            part = jnp.zeros((LAT, CELLS), F32)
            for dy in range(3):
                tap = (dy * 3 + dx) * LAT
                piece = joint[tap : tap + LAT]
                if dy != 1:
                    piece = pltpu.roll(piece, (-(dy - 1) * SIDE) % CELLS, 1)
                    inside = (row >= 1) if dy == 0 else (row <= SIDE - 2)
                    piece = jnp.where(inside, piece, 0.0)
                part = part + piece
            if dx != 1:
                part = pltpu.roll(part, (-(dx - 1)) % CELLS, 1)
                inside = (col >= 1) if dx == 0 else (col <= SIDE - 2)
                part = jnp.where(inside, part, 0.0)
            result = result + part
        results.append(result.astype(BF16))
    sorted_cells = nn(jnp.concatenate(results, axis=0), cell_order()).astype(BF16)
    for ab in range(4):
        out[ab * LAT : (ab + 1) * LAT, :] = jnp.concatenate(
            [
                sorted_cells[f * LAT : (f + 1) * LAT, ab * 64 : (ab + 1) * 64]
                for f in range(FRAMES)
            ],
            axis=1,
        )


def shift_row(m_hi, m_lo, part):
    unit = jnp.where(lax.broadcasted_iota(jnp.int32, (16, AUG), 1) == FEAT + 1, 1.0, 0.0).astype(BF16)
    return (nt(unit, m_hi[part, :]) + nt(unit, m_lo[part, :]))[0:1]


def stacked(value):
    return jnp.concatenate([value[:, i : i + 128] for i in range(0, value.shape[1], 128)], axis=0)


def share_kernel(pair, one, two, three, out, total):
    value = (pair[...].astype(F32) + two[...].astype(F32)) + (one[...].astype(F32) + three[...].astype(F32))
    total[...] = value
    for j in range(out.shape[0]):
        out[j] = value.astype(BF16)


def cotangent_kernel(grad0, grad1, grad2, grad3, other0, other1, other2, other3, gate, w_out, lat_sorted, d_attn, d_out, latents):
    place = lax.axis_index("mp")
    core, level = lax.rem(place, 2), lax.div(place, 2)
    total = jnp.zeros((ROWS, HEADS * HD), F32)
    for k, grads in enumerate(((grad0, other0), (grad1, other1), (grad2, other2), (grad3, other3))):
        for side in range(2):
            m = lax.rem(level - k + 4, 4) * 2 + (core if side == 0 else 1 - core)
            cols = pl.ds(pl.multiple_of(m * 384, 128), 384)
            part = (grads[side][...].astype(F32) * gate[:, cols]).astype(BF16)
            d_attn[m] = part
            total = total + nt(part, w_out[:, cols])
    d_out[...] = total.astype(BF16)
    by_frame = jnp.concatenate(
        [
            jnp.concatenate(
                [lat_sorted[ab * LAT : (ab + 1) * LAT, f * 64 : (f + 1) * 64] for ab in range(4)], axis=1
            )
            for f in range(FRAMES)
        ],
        axis=0,
    )
    hi, lo = hi_lo(by_frame)
    order = cell_order()
    values = nt(hi, order) + nt(lo, order)
    for f in range(FRAMES):
        latents[f] = values[f * LAT : (f + 1) * LAT]


def prepare_kernel(
    embed_w,
    embed_b,
    shift,
    scale,
    w_hbm,
    gram_hi,
    gram_lo,
    m_hi,
    m_lo,
    m_k,
    centered_two,
    own_rows,
    window,
    w_qkv,
    arrived,
):
    fetch = pltpu.make_async_copy(w_hbm, w_qkv, arrived)
    fetch.start()
    row = lax.broadcasted_iota(jnp.int32, (16, D), 0)
    extra = jnp.where(row == 0, embed_b[...], 0.0)
    augmented = jnp.concatenate([nn(turn_back(), embed_w[...]), extra], axis=0)
    centered = augmented - jnp.mean(augmented, axis=1, keepdims=True)
    c_hi, c_lo = hi_lo(centered)
    centered_two[:AUG, :] = c_hi
    centered_two[AUG:, :] = c_lo
    gram = (nt(c_hi, c_hi) + nt(c_hi, c_lo) + nt(c_lo, c_hi)) * (1.0 / D)
    g_hi, g_lo = hi_lo(gram)
    gram_hi[...] = g_hi
    gram_lo[...] = g_lo
    row = lax.broadcasted_iota(jnp.int32, (AUG, D), 0)
    modulated = jnp.where(row == FEAT + 1, shift[...], centered * (1.0 + scale[...]))
    a_hi, a_lo = hi_lo(modulated)
    fetch.wait()
    both = nn(jnp.concatenate([a_hi, a_lo], axis=0), w_qkv[...])
    turned = (both[:AUG] + both[AUG:]).T
    t_hi, t_lo = hi_lo(turned)
    m_hi[...] = t_hi
    m_lo[...] = t_lo
    for h in range(HEADS):
        keys = slice(h * 384 + 128, h * 384 + 256)
        m_k[h * HD : (h + 1) * HD, :] = jnp.concatenate([t_hi[keys], t_hi[keys], t_lo[keys]], axis=1)
    window[...] = modulated.T
    slab = lax.axis_index("slab")
    o_hi, o_lo = hi_lo(window[pl.ds(pl.multiple_of(slab * 192, 64), 192), :])
    own_rows[...] = jnp.concatenate([o_hi, o_lo], axis=1)


def forward_kernel(
    frames,
    res,
    patches,
    place,
    gram_hi,
    gram_lo,
    m_k,
    m_hi,
    m_lo,
    d_out,
    q_gain,
    k_gain,
    grad_out,
    w_out,
    d_attn,
    embed_w,
    embed_b,
    gate,
    attn_mine,
    attn_other,
    g_part0,
    g_part1,
    g_part2,
    g_part3,
    hidden_cols,
    early,
    g_own,
    gate_cols,
    s_t,
    k_t,
    rk_t,
    q_ext,
    q_norm,
    q_facts,
    u_cat,
    s_own,
):
    blocks = patches.shape[0]
    row_aug = lax.broadcasted_iota(jnp.int32, (AUG, ROWS), 0)
    row16 = lax.broadcasted_iota(jnp.int32, (16, ROWS), 0)
    token = lax.broadcasted_iota(jnp.int32, (1, ROWS), 1)
    position = lax.broadcasted_iota(jnp.int32, (ROWS, ROWS), 0).astype(F32)
    base = (lax.axis_index("slab") * ROWS).astype(F32)
    k_gain_c = column(k_gain[...])
    one_row = jnp.where(row16 == 0, 1.0, 0.0).astype(BF16)

    def prepare(j, carry):
        x_q, clip_q = carry
        block = pl.ds(pl.multiple_of(j * ROWS, ROWS), ROWS)
        x_aug = jnp.concatenate([patches[j], one_row], axis=0)
        x_f = x_aug.astype(F32)
        gx = nn(gram_hi[...], x_aug) + nn(gram_lo[...], x_aug)
        rstd = lax.rsqrt(jnp.sum(gx * x_f, axis=0, keepdims=True) + EPSILON)
        s_hi, s_lo = hi_lo(jnp.where(row_aug == FEAT + 1, 1.0, x_f * rstd))
        s_t[:AUG, block] = s_hi
        s_t[AUG:, block] = s_lo
        clip = clip_number(frames, j * FRAMES + (token >> 6))
        height = jnp.zeros((1, ROWS), jnp.int32)
        width = jnp.zeros((1, ROWS), jnp.int32)
        for c in range(CLIPS):
            height = jnp.where(clip == c, res[c : c + 1, 0:1], height)
            width = jnp.where(clip == c, res[c : c + 1, 1:2], width)
        valid = (2 * ((token >> 3) & 7) < height) & (2 * (token & 7) < width)
        member = row16 == clip
        mask = jnp.where((row16 < CLIPS) & ~(member & valid), OFF, 0.0).astype(BF16)
        both = nn(m_k[...], jnp.concatenate([s_hi, s_lo, s_hi], axis=0))
        for h in range(HEADS):
            k = both[h * HD : (h + 1) * HD]
            rk = lax.rsqrt(jnp.mean(k * k, axis=0, keepdims=True) + EPSILON)
            rk_t[h, :, block] = jnp.broadcast_to(rk, (8, ROWS))
            k_t[h, :HD, block] = (k * rk * k_gain_c).astype(BF16)
            k_t[h, HD:, block] = mask
        spot = jnp.concatenate([place[j, 4:5, :], place[j, 5:6, :]], axis=1)
        chosen = jnp.where(spot == position + base, 1.0, 0.0).astype(BF16)
        x_q = x_q + nt(chosen, x_aug)
        clip_q = clip_q + nt(chosen, jnp.where(member, 1.0, 0.0).astype(BF16))
        return x_q, clip_q

    x_q, clip_q = lax.fori_loop(
        0, blocks, prepare, (jnp.zeros((ROWS, AUG), F32), jnp.zeros((ROWS, 16), F32)), unroll=PREPARE_UNROLL
    )
    x_qb = x_q.astype(BF16)
    own_cols = pl.ds(pl.multiple_of(lax.axis_index("mp") * 384, 128), 384)
    gate_cols[...] = gate[:, own_cols]
    embed_cols = nn(turn_back(), embed_w.ready()[:, own_cols]).astype(BF16)
    hidden_cols[...] = (nn(x_qb[:, :FEAT], embed_cols) + embed_b[:, own_cols]).astype(BF16)
    g_own[...] = stacked(nn(turn_rows(AUG), tn(x_qb, grad_out.ready()[...]).astype(BF16)))
    gx_q = nn(x_qb, gram_hi[...]) + nn(x_qb, gram_lo[...])
    rstd_q = lax.rsqrt(jnp.sum(gx_q * x_q, axis=1, keepdims=True) + EPSILON)
    lane_aug = lax.broadcasted_iota(jnp.int32, (ROWS, AUG), 1)
    s_q = jnp.where(lane_aug == FEAT + 1, 1.0, x_q * rstd_q)
    s_own[...] = s_q
    s_qhi, s_qlo = hi_lo(s_q)
    clip_qb = clip_q.astype(BF16)
    lane = lax.broadcasted_iota(jnp.int32, (ROWS, 128), 1)
    facts = jnp.zeros((ROWS, 128), F32)
    for h in range(HEADS):
        mine = slice(h * 384, h * 384 + 128)
        q = nt(s_qhi, m_hi[mine, :]) + nt(s_qlo, m_hi[mine, :]) + nt(s_qhi, m_lo[mine, :])
        rq = lax.rsqrt(jnp.mean(q * q, axis=1, keepdims=True) + EPSILON)
        qn = q * rq
        q_norm[h] = qn
        q_ext[h, :, :HD] = (qn * (q_gain[...] * (HD**-0.5 * LOG2E))).astype(BF16)
        q_ext[h, :, HD:] = clip_qb
        facts = jnp.where(lane == h, rq, facts)

    def forward(j, totals):
        block = pl.ds(pl.multiple_of(j * FWD_BLOCK, FWD_BLOCK), FWD_BLOCK)
        s_block = s_t[:, block]
        probs = [jnp.exp2(nn(q_ext[h], k_t[h, :, block])).astype(BF16) for h in range(HEADS)]
        return tuple(totals[h] + nt(probs[h], s_block) for h in range(HEADS))

    totals = lax.fori_loop(
        0, 4096 // FWD_BLOCK, forward, (jnp.zeros((ROWS, 2 * AUG), F32),) * HEADS, unroll=FWD_UNROLL
    )
    heads = []
    d_out = d_out.ready()
    for h in range(HEADS):
        inv_l = 1.0 / totals[h][:, FEAT + 1 : FEAT + 2]
        z_hi, z_lo = hi_lo((totals[h][:, :AUG] + totals[h][:, AUG:]) * inv_l)
        mine = slice(h * 384 + 256, h * 384 + 384)
        att = (nt(z_hi, m_hi[mine, :]) + nt(z_lo, m_hi[mine, :]) + nt(z_hi, m_lo[mine, :])).astype(BF16)
        heads.append(att)
        d_bf = d_out[:, h * HD : (h + 1) * HD]
        early[:, h * HD : (h + 1) * HD] = tn(z_hi, d_bf)
        do = d_bf.astype(F32)
        shift_v = shift_row(m_hi, m_lo, mine)
        weight = jnp.sum(do * (att.astype(F32) - shift_v), axis=1, keepdims=True) * inv_l
        facts = jnp.where(lane == 2 + h, weight, facts)
        u = (nn(d_bf, m_hi[mine, :]) + nn(d_bf, m_lo[mine, :])) * inv_l
        u_hi, u_lo = hi_lo(jnp.where(lane_aug == FEAT + 1, 0.0, u))
        u_cat[h] = jnp.concatenate([u_hi, u_lo, u_hi], axis=1)
    q_facts[...] = facts
    att_all = jnp.concatenate(heads, axis=1)
    place_mp, slab = lax.axis_index("mp"), lax.axis_index("slab")
    core = lax.rem(place_mp, 2)
    y_pos, x_pos = lax.div(slab, 4), lax.rem(slab, 4)
    d_attn, w_out = d_attn.ready(), w_out.ready()
    for k, g_part in enumerate((g_part0, g_part1, g_part2, g_part3)):
        y_to = lax.rem(y_pos + k, 4)
        for half in range(2):
            both = tn(d_attn[2 * y_to + half], att_all).astype(BF16)
            for side in range(2):
                slot = lax.rem(2 * half + side - x_pos + 4, 4)
                g_part.buffer[slot] = both[side * 192 : (side + 1) * 192]
        g_part.send()
    for side, attn_part in enumerate((attn_other, attn_mine)):
        for k in range(4):
            m = 2 * k + (core if side == 1 else 1 - core)
            cols = pl.ds(pl.multiple_of(m * 384, 128), 384)
            attn_part.buffer[k] = nn(att_all, w_out[:, cols]).astype(BF16)
        attn_part.send()


def backward_kernel(
    s_t,
    k_t,
    rk_t,
    q_ext,
    q_norm,
    q_facts,
    u_cat,
    s_own,
    m_hi,
    m_lo,
    q_gain,
    k_gain,
    early,
    mod_scale,
    centered,
    w_qkv,
    sums,
    y_mine,
    y_other,
    q_t,
):
    shift_k = []
    for h in range(HEADS):
        q_t[h] = q_ext[h, :, :HD].astype(F32).T.astype(BF16)
        mine = slice(h * 384 + 128, h * 384 + 256)
        shift_k.append(
            m_hi[mine, FEAT + 1 : FEAT + 2].astype(F32) + m_lo[mine, FEAT + 1 : FEAT + 2].astype(F32)
        )
    k_gain_c = column(k_gain[...])
    gain_back = k_gain_c * (1.0 / LOG2E)
    gain_inv = 1.0 / k_gain_c
    weights = [q_facts[:, 2 + h : 3 + h] for h in range(HEADS)]

    def backward(j, carry):
        grad_qs, p_k, quad = carry
        block = pl.ds(pl.multiple_of(j * BWD_BLOCK, BWD_BLOCK), BWD_BLOCK)
        s_hi = s_t[:AUG, block]
        s_cat = jnp.concatenate([s_hi, s_hi, s_t[AUG:, block]], axis=0)
        m2 = jnp.zeros((1, BWD_BLOCK), F32)
        new_q, dks = [], []
        for h in range(HEADS):
            keys = k_t[h, :HD, block]
            p = jnp.exp2(nn(q_ext[h], k_t[h, :, block]))
            raw = p * nn(u_cat[h], s_cat)
            m2 = m2 + jnp.sum(raw, axis=0, keepdims=True)
            d_score = (raw - p * weights[h]).astype(BF16)
            new_q.append(grad_qs[h] + nt(d_score, keys))
            scaled = nn(q_t[h], d_score) * gain_back
            kn = keys.astype(F32) * gain_inv
            rk = rk_t[h, 0:1, block]
            dk = rk * (scaled - kn * jnp.mean(scaled * kn, axis=0, keepdims=True))
            m2 = m2 + jnp.sum(dk * (kn * (1.0 / rk) - shift_k[h]), axis=0, keepdims=True)
            dks.append(dk.astype(BF16))
        p_k = p_k + nt(s_hi, jnp.concatenate(dks, axis=0))
        quad = quad + nt((s_hi.astype(F32) * m2).astype(BF16), s_hi)
        return tuple(new_q), p_k, quad

    grad_qs, p_k, quad = lax.fori_loop(
        0,
        4096 // BWD_BLOCK,
        backward,
        (
            (jnp.zeros((ROWS, HD), F32),) * HEADS,
            jnp.zeros((AUG, HEADS * HD), F32),
            jnp.zeros((AUG, AUG), F32),
        ),
        unroll=BWD_UNROLL,
    )
    s_q = s_own[...]
    s_qhi = s_q.astype(BF16)
    m2_q = jnp.zeros((ROWS, 1), F32)
    pieces = []
    for h in range(HEADS):
        mine = slice(h * 384, h * 384 + 128)
        rq = q_facts[:, h : h + 1]
        qn = q_norm[h]
        scaled = grad_qs[h] * (q_gain[...] * HD**-0.5)
        dq = rq * (scaled - qn * jnp.mean(scaled * qn, axis=1, keepdims=True))
        shift_q = shift_row(m_hi, m_lo, mine)
        m2_q = m2_q + jnp.sum(dq * (qn * (1.0 / rq) - shift_q), axis=1, keepdims=True)
        pieces += [tn(s_qhi, dq.astype(BF16)), p_k[:, h * HD : (h + 1) * HD], early[:, h * HD : (h + 1) * HD]]
    p_rows = jnp.concatenate(pieces, axis=1)
    p_all = p_rows.astype(BF16)
    extra = [p_rows[FEAT + i : FEAT + 1 + i, g * 128 : (g + 1) * 128] for i in range(2) for g in range(6)]
    extra = jnp.concatenate(extra + [jnp.zeros((4, 128), F32)], axis=0)
    sums[:384, :] = stacked(p_all[:FEAT])
    sums[384:, :] = extra.astype(BF16)
    quad = ((quad + tn((s_q * m2_q).astype(BF16), s_qhi)) * (1.0 / D)).astype(BF16)
    turn = turn_rows(AUG)
    turned = nn(turn, p_all).astype(BF16)
    quad = nn(turn, quad).astype(BF16)
    w_qkv = w_qkv.ready()
    back = nt(turned, w_qkv[...]) * (1.0 + mod_scale[...])
    back = back - jnp.mean(back, axis=1, keepdims=True)
    back = (back - nn(jnp.concatenate([quad, quad], axis=1), centered[...])).astype(BF16)
    place = lax.axis_index("mp")
    core, level = lax.rem(place, 2), lax.div(place, 2)
    for z in range(4):
        slot = lax.rem(z - level + 4, 4)
        even = back[:, 2 * z * 384 : (2 * z + 1) * 384]
        odd = back[:, (2 * z + 1) * 384 : (2 * z + 2) * 384]
        y_mine[slot] = stacked(jnp.where(core == 0, even, odd))
        y_other[slot] = stacked(jnp.where(core == 0, odd, even))


def attention_kernel(
    frames,
    res,
    patches,
    place,
    gram_hi,
    gram_lo,
    m_k,
    m_hi,
    m_lo,
    d_out,
    q_gain,
    k_gain,
    grad_out,
    w_out,
    d_attn,
    embed_w,
    embed_b,
    gate,
    mod_scale,
    centered,
    w_qkv,
    attn_mine,
    attn_other,
    g_part0,
    g_part1,
    g_part2,
    g_part3,
    hidden_cols,
    g_own,
    gate_cols,
    sums,
    y_mine,
    y_other,
    early,
    s_t,
    k_t,
    rk_t,
    q_ext,
    q_norm,
    q_facts,
    u_cat,
    s_own,
    q_t,
):
    forward_kernel(
        frames,
        res,
        patches,
        place,
        gram_hi,
        gram_lo,
        m_k,
        m_hi,
        m_lo,
        d_out,
        q_gain,
        k_gain,
        grad_out,
        w_out,
        d_attn,
        embed_w,
        embed_b,
        gate,
        attn_mine,
        attn_other,
        g_part0,
        g_part1,
        g_part2,
        g_part3,
        hidden_cols,
        early,
        g_own,
        gate_cols,
        s_t,
        k_t,
        rk_t,
        q_ext,
        q_norm,
        q_facts,
        u_cat,
        s_own,
    )
    backward_kernel(
        s_t,
        k_t,
        rk_t,
        q_ext,
        q_norm,
        q_facts,
        u_cat,
        s_own,
        m_hi,
        m_lo,
        q_gain,
        k_gain,
        early,
        mod_scale,
        centered.ready(),
        w_qkv,
        sums,
        y_mine,
        y_other,
        q_t,
    )


def weights_kernel(own, one, two, three, own_rows, g_qkv, g_embed):
    total = (own[...].astype(F32) + two[...].astype(F32)) + (one[...].astype(F32) + three[...].astype(F32))
    row = lax.broadcasted_iota(jnp.int32, (AUG, 128), 0)
    blocks = []
    for g in range(6):
        block = jnp.concatenate([total[g * 64 : (g + 1) * 64], jnp.zeros((AUG - FEAT, 128), F32)], axis=0)
        block = jnp.where(row == FEAT, total[384 + g : 385 + g], block)
        blocks.append(jnp.where(row == FEAT + 1, total[390 + g : 391 + g], block))
    p_all = jnp.concatenate(blocks, axis=1).astype(BF16)
    g_qkv[...] = nn(own_rows[...], jnp.concatenate([p_all, p_all], axis=0))
    for g in range(3):
        g_embed[:, g * 128 : (g + 1) * 128] = total[400 + g * 64 : 464 + g * 64]


VMEM = pl.BlockSpec(memory_space=pltpu.VMEM)
SMEM = pl.BlockSpec(memory_space=pltpu.SMEM)
ANY = pl.BlockSpec(memory_space=pl.ANY)


class Fetched:
    def __init__(self, source, buffer, sem):
        self.buffer, self.copy = buffer, pltpu.make_async_copy(source, buffer, sem)
        self.copy.start()

    def ready(self):
        self.copy.wait()
        return self.buffer


class Sent:
    def __init__(self, target, buffer, sem):
        self.buffer, self.copy = buffer, pltpu.make_async_copy(buffer, target, sem)

    def send(self):
        self.copy.start()


def call(kernel, inputs, outputs, scratch, flops, mib, places, out_places=None):
    single = not isinstance(outputs, tuple)
    outs = (outputs,) if single else outputs
    out_places = out_places or "v" * len(outs)
    staged = [
        (i, pltpu.VMEM(v.shape, v.dtype)) for i, (p, v) in enumerate(zip(places, inputs, strict=True)) if p == "l"
    ]
    sent = [(i, pltpu.VMEM(o.shape, o.dtype)) for i, (p, o) in enumerate(zip(out_places, outs, strict=True)) if p == "e"]
    n_in, n_out, n_stage, n_sent = len(inputs), len(outs), len(staged), len(sent)

    def wrapped(*refs):
        ins, results = list(refs[:n_in]), list(refs[n_in : n_in + n_out])
        rest = refs[n_in + n_out :]
        buffers, rest = rest[:n_stage], rest[n_stage:]
        holds, rest = rest[:n_sent], rest[n_sent:]
        sems, rest = rest[: n_stage + n_sent], rest[n_stage + n_sent :]
        for slot, (i, _) in enumerate(staged):
            ins[i] = Fetched(ins[i], buffers[slot], sems[slot])
        for slot, (i, _) in enumerate(sent):
            results[i] = Sent(results[i], holds[slot], sems[n_stage + slot])
        kernel(*ins, *results, *rest)
        for i, _ in sent:
            results[i].copy.wait()

    specs = {"v": VMEM, "e": ANY, "l": ANY, "r": ANY, "s": SMEM}
    result = pl.pallas_call(
        wrapped,
        out_shape=outs,
        in_specs=[specs[p] for p in places],
        out_specs=tuple(specs[p] for p in out_places),
        scratch_shapes=[b for _, b in staged]
        + [b for _, b in sent]
        + [pltpu.SemaphoreType.DMA] * (n_stage + n_sent)
        + scratch,
        compiler_params=pltpu.CompilerParams(vmem_limit_bytes=mib * MIB),
        cost_estimate=pl.CostEstimate(flops=flops, bytes_accessed=1 << 20, transcendentals=0),
    )(*inputs)
    return result[0] if single else result


def shift_by(value, axis, move):
    return lax.ppermute(value, axis, [(i, move(i)) for i in range(lax.axis_size(axis))])


def along_x(k):
    return lambda i: (i // 4) * 4 + (i % 4 + k) % 4


def along_y(k):
    return lambda i: ((i // 4 + k) % 4) * 4 + i % 4


def along_z(k):
    return lambda i: ((i // 2 + k) % 4) * 2 + i % 2


def sum_of_four(value, axis, move, kind):
    sent = value.astype(kind)
    one, two, three = (shift_by(sent, axis, move(k)).astype(F32) for k in (1, 2, 3))
    return (sent.astype(F32) + two) + (one + three)


Z_GROUPS = [[0, 2, 4, 6], [1, 3, 5, 7]]


def level_sum(pair):
    one, two, three = (shift_by(pair[k], "mp", along_z(k)).astype(F32) for k in (1, 2, 3))
    return (pair[0].astype(F32) + two) + (one + three)


def body(
    enc_feat,
    gn_gain,
    gn_bias,
    conv_w,
    clip_frames,
    clip_res,
    token_place,
    embed_w,
    embed_b,
    mod_shift,
    mod_scale,
    mod_gate,
    w_qkv,
    q_gain,
    k_gain,
    w_out,
    grad_out,
):
    slabs = lax.axis_size("slab")
    mp_size = lax.axis_size("mp")
    cols_dev = D // mp_size
    row_cols = D // slabs

    clip_res = jnp.pad(clip_res, ((0, 4), (0, 126)))
    all_sent = call(
        stats_kernel,
        (clip_frames, clip_res, enc_feat, token_place.reshape(2, 128)),
        jax.ShapeDtypeStruct((slabs, 8, 128), F32),
        [],
        1 << 20,
        60,
        "svvv",
    )
    all_stats = lax.all_to_all(all_sent, "slab", split_axis=0, concat_axis=0, tiled=True)
    rim = shift_by(enc_feat[FRAMES - 2 :], "slab", lambda i: (i + 1) % slabs)
    rim, grad_sent = lax.optimization_barrier((rim, grad_out))
    grads = (grad_sent,) + tuple(shift_by(grad_sent, "mp", along_z(k)) for k in (1, 2, 3))
    taps = call(
        taps_kernel,
        (conv_w,),
        jax.ShapeDtypeStruct((432, FEAT), BF16),
        [],
        1 << 33,
        60,
        "v",
    )
    partial = call(
        conv_kernel,
        (clip_frames, clip_res, enc_feat, rim, all_stats, gn_gain[None, :], gn_bias[None, :], taps),
        jax.ShapeDtypeStruct((FEAT, CELLS), BF16),
        [pltpu.VMEM((FRAMES + 2, 432, CELLS), F32)],
        1 << 28,
        60,
        "svvvvvvv",
    )
    partial, grads = lax.optimization_barrier((partial, grads))
    pair = (partial.astype(F32) + shift_by(partial, "mp", lambda i: i ^ 1).astype(F32)).astype(BF16)
    patches_sent, lat_sorted = call(
        share_kernel,
        (pair,) + tuple(shift_by(pair, "mp", along_z(k)) for k in (1, 2, 3)),
        (
            jax.ShapeDtypeStruct((slabs, FEAT, CELLS), BF16),
            jax.ShapeDtypeStruct((FEAT, CELLS), F32),
        ),
        [],
        1 << 20,
        4,
        "vvvv",
    )
    all_patches = lax.all_to_all(patches_sent, "slab", split_axis=0, concat_axis=0, tiled=True)

    embed_late, _ = lax.optimization_barrier((embed_b, patches_sent))
    gram_hi, gram_lo, m_hi, m_lo, m_k, centered, own_rows = call(
        prepare_kernel,
        (embed_w, embed_late[None, :], mod_shift[None, :], mod_scale[None, :], w_qkv),
        (
            jax.ShapeDtypeStruct((AUG, AUG), BF16),
            jax.ShapeDtypeStruct((AUG, AUG), BF16),
            jax.ShapeDtypeStruct((768, AUG), BF16),
            jax.ShapeDtypeStruct((768, AUG), BF16),
            jax.ShapeDtypeStruct((HEADS * HD, 3 * AUG), BF16),
            jax.ShapeDtypeStruct((2 * AUG, D), BF16),
            jax.ShapeDtypeStruct((row_cols, 2 * AUG), BF16),
        ),
        [pltpu.VMEM((D, AUG), F32), pltpu.VMEM((D, 768), BF16), pltpu.SemaphoreType.DMA],
        1 << 32,
        60,
        "vvvvr",
    )

    grads, lat_sorted = lax.optimization_barrier((grads, lat_sorted))
    others = tuple(shift_by(block, "mp", lambda i: i ^ 1) for block in grads)
    d_attn, d_out, latents = call(
        cotangent_kernel,
        (*grads, *others, mod_gate[None, :], w_out, lat_sorted),
        (
            jax.ShapeDtypeStruct((mp_size, ROWS, cols_dev), BF16),
            jax.ShapeDtypeStruct((ROWS, HEADS * HD), BF16),
            jax.ShapeDtypeStruct((FRAMES, LAT, CELLS), F32),
        ),
        [],
        1 << 32,
        60,
        "vvvvvvvvvvv",
    )

    attn_mine, attn_other, *g_parts, hidden_cols, g_own, gate_cols, sums, y_mine, y_other = call(
        attention_kernel,
        (
            clip_frames,
            clip_res,
            all_patches,
            all_stats,
            gram_hi,
            gram_lo,
            m_k,
            m_hi,
            m_lo,
            d_out,
            q_gain[None, :],
            k_gain[None, :],
            grad_out,
            w_out,
            d_attn,
            embed_w,
            embed_b[None, :],
            mod_gate[None, :],
            mod_scale[None, :],
            centered,
            w_qkv,
        ),
        (
            *(jax.ShapeDtypeStruct((4, ROWS, cols_dev), BF16),) * 2,
            *(jax.ShapeDtypeStruct((4, row_cols, HEADS * HD), BF16),) * 4,
            jax.ShapeDtypeStruct((ROWS, cols_dev), BF16),
            jax.ShapeDtypeStruct((192, 128), F32),
            jax.ShapeDtypeStruct((1, cols_dev), F32),
            jax.ShapeDtypeStruct((400, 128), BF16),
            jax.ShapeDtypeStruct((4, 192, 128), BF16),
            jax.ShapeDtypeStruct((4, 192, 128), BF16),
        ),
        [
            pltpu.VMEM((AUG, 256), F32),
            pltpu.VMEM((2 * AUG, 4096), BF16),
            pltpu.VMEM((HEADS, EXT, 4096), BF16),
            pltpu.VMEM((HEADS, 8, 4096), F32),
            pltpu.VMEM((HEADS, ROWS, EXT), BF16),
            pltpu.VMEM((HEADS, ROWS, HD), F32),
            pltpu.VMEM((ROWS, 128), F32),
            pltpu.VMEM((HEADS, ROWS, 3 * AUG), BF16),
            pltpu.VMEM((ROWS, AUG), F32),
            pltpu.VMEM((HEADS, HD, ROWS), BF16),
        ],
        1 << 34,
        60,
        "svvvvvvvvlvvllllvvvll",
        "eeeeeevvvvvv",
    )

    y_got = shift_by(y_other, "mp", lambda i: i ^ 1)
    y_pair = (y_mine.astype(F32) + y_got.astype(F32)).astype(BF16)
    y_pair, attn_other, g_parts = lax.optimization_barrier((y_pair, attn_other, g_parts))
    attn_got = shift_by(attn_other, "mp", lambda i: i ^ 1)
    g_one, g_two, g_three = (shift_by(g_parts[k], "slab", along_y(k)) for k in (1, 2, 3))
    embed_part = level_sum(y_pair) + g_own
    payload = jnp.concatenate([sums, embed_part.astype(BF16)], axis=0)
    payload, attn_mine = lax.optimization_barrier((payload, attn_mine))
    sent = tuple(shift_by(payload, "slab", along_x(k)) for k in (1, 2, 3))
    sent, g_one, g_two, g_three = lax.optimization_barrier((sent, g_one, g_two, g_three))
    total = (
        (payload.astype(F32) + sent[1].astype(F32)) + (sent[0].astype(F32) + sent[2].astype(F32))
    ).astype(BF16)
    attn_pair = (attn_mine.astype(F32) + attn_got.astype(F32)).astype(BF16)
    attn_got = lax.all_to_all(attn_pair, "mp", split_axis=0, concat_axis=0, tiled=True, axis_index_groups=Z_GROUPS)
    total, attn_got = lax.optimization_barrier((total, attn_got))
    received = tuple(shift_by(total, "slab", along_y(k)) for k in (1, 2, 3))
    total, g_two = lax.optimization_barrier((total, g_two))
    g_sum = (
        (g_parts[0].astype(F32) + g_two.astype(F32)) + (g_one.astype(F32) + g_three.astype(F32))
    ).astype(BF16)
    g_got = tuple(shift_by(g_sum[k], "slab", along_x(k)) for k in (1, 2, 3))
    received, g_late = lax.optimization_barrier((received, g_sum[0]))
    attn_cols = jnp.sum(attn_got.astype(F32), axis=0)
    block_out = (hidden_cols.astype(F32) + gate_cols * attn_cols).astype(BF16)
    g_out = (
        (g_late.astype(F32) + g_got[1].astype(F32)) + (g_got[0].astype(F32) + g_got[2].astype(F32))
    ).T
    g_qkv, g_embed = call(
        weights_kernel,
        (total, *received, own_rows),
        (
            jax.ShapeDtypeStruct((row_cols, 768), F32),
            jax.ShapeDtypeStruct((FEAT, cols_dev), F32),
        ),
        [],
        1 << 26,
        4,
        "vvvvv",
    )
    return (latents, block_out, g_qkv, g_out, g_embed)


def solution(mesh):
    in_specs = (
        P(("dp", "slab"), "mp", None),
        P("mp"),
        P("mp"),
        P("mp", None),
        P("dp"),
        P("dp", None),
        P(("dp", "slab")),
        P(),
        P(),
        P("dp"),
        P("dp"),
        P("dp"),
        P(None, "mp"),
        P(),
        P(),
        P("mp", None),
        P(("dp", "slab"), "mp"),
    )
    out_specs = (
        P(("dp", "slab"), None, None),
        P(("dp", "slab"), "mp"),
        P(("dp", "slab"), "mp"),
        P(("dp", "mp"), "slab"),
        P("dp", "mp"),
    )
    return jax.shard_map(body, mesh=mesh, in_specs=in_specs, out_specs=out_specs, check_vma=False)
```

```python
import functools

import jax
import jax.numpy as jnp
from jax import lax
from jax.experimental import pallas as pl
from jax.experimental.pallas import tpu as pltpu
from jax.sharding import PartitionSpec as P

D = 3072
HD = 128
LAT = 16
CLIPS = 4
SIDE = 16
PSIDE = 8
CELLS = 256
GS = 16
HEADS = 2
ROWS = 256
FRAMES = 4
FEAT = 64
AUG = 80
EXT = 144
EPSILON = 1e-06
HIGHEST = lax.Precision.HIGHEST
LOG2E = 1.4426950408889634
OFF = -1e30
F32 = jnp.float32
BF16 = jnp.bfloat16
MIB = 1024 * 1024
PREPARE_UNROLL = 4
FWD_BLOCK = 1024
FWD_UNROLL = 1
BWD_BLOCK = 1024
BWD_UNROLL = 2


def nn(a, b):
    return lax.dot_general(a, b, (((1,), (0,)), ((), ())), preferred_element_type=F32)


def nt(a, b):
    return lax.dot_general(a, b, (((1,), (1,)), ((), ())), preferred_element_type=F32)


def tn(a, b):
    return lax.dot_general(a, b, (((0,), (0,)), ((), ())), preferred_element_type=F32)


def hi_lo(value):
    hi = value.astype(BF16)
    return hi, (value - hi.astype(F32)).astype(BF16)


def clip_number(frames, frame):
    one = frames[0]
    two = one + frames[1]
    three = two + frames[2]
    return (
        jnp.where(frame >= one, 1, 0) + jnp.where(frame >= two, 1, 0) + jnp.where(frame >= three, 1, 0)
    )


def frame_facts(frames, res, frame):
    clip = clip_number(frames, frame)
    one = frames[0]
    two = one + frames[1]
    three = two + frames[2]
    start = jnp.where(
        clip == 0, 0, jnp.where(clip == 1, one, jnp.where(clip == 2, two, three))
    )
    height, width = res[3:4, 0:1], res[3:4, 1:2]
    for c in range(CLIPS - 1):
        height = jnp.where(clip == c, res[c : c + 1, 0:1], height)
        width = jnp.where(clip == c, res[c : c + 1, 1:2], width)
    return clip, start, height, width


def column(row):
    return jnp.broadcast_to(row, (8, row.shape[1])).T[:, :1]


def turn_rows(width):
    feat = lax.broadcasted_iota(jnp.int32, (FEAT, width), 0)
    other = lax.broadcasted_iota(jnp.int32, (FEAT, width), 1)
    return jnp.where((feat & 3) * LAT + (feat >> 2) == other, 1.0, 0.0).astype(BF16)


def turn_back():
    feat = lax.broadcasted_iota(jnp.int32, (FEAT, FEAT), 0)
    other = lax.broadcasted_iota(jnp.int32, (FEAT, FEAT), 1)
    return jnp.where((feat & 15) * 4 + (feat >> 4) == other, 1.0, 0.0).astype(BF16)


def cell_order():
    cell = lax.broadcasted_iota(jnp.int32, (CELLS, CELLS), 0)
    place = lax.broadcasted_iota(jnp.int32, (CELLS, CELLS), 1)
    row, col = cell >> 4, cell & 15
    spot = ((row & 1) * 2 + (col & 1)) * 64 + (row >> 1) * PSIDE + (col >> 1)
    return jnp.where(spot == place, 1.0, 0.0).astype(BF16)


def cell_valid(height, width):
    cell = lax.broadcasted_iota(jnp.int32, (1, CELLS), 1)
    return ((cell >> 4) < height) & ((cell & 15) < width)


def stats_kernel(frames, res, enc, place, out):
    slab = lax.axis_index("slab")
    lane = lax.broadcasted_iota(jnp.int32, (FEAT, 128), 1)
    total = jnp.zeros((FEAT, 128), F32)
    for f in range(FRAMES):
        clip, _, height, width = frame_facts(frames, res, slab * FRAMES + f)
        kept = jnp.where(cell_valid(height, width), enc[f].astype(F32), 0.0)
        sums = jnp.sum(kept, axis=1, keepdims=True)
        squares = jnp.sum(kept * kept, axis=1, keepdims=True)
        total = total + jnp.where(lane == clip, sums, 0.0) + jnp.where(lane == clip + 4, squares, 0.0)
    groups = [jnp.sum(total[g * GS : (g + 1) * GS], axis=0, keepdims=True) for g in range(4)]
    payload = jnp.concatenate(groups + [place[...].astype(F32), jnp.zeros((2, 128), F32)], axis=0)
    for j in range(out.shape[0]):
        out[j] = payload


def taps_kernel(taps, out):
    out[...] = taps[...].astype(F32).T.astype(BF16)


def conv_kernel(frames, res, enc, rim, sums, gain, bias, taps, out, proj):
    totals = jnp.sum(sums[...], axis=0)
    lane = lax.broadcasted_iota(jnp.int32, (8, 128), 1)
    first = lax.axis_index("slab") * FRAMES
    gain_c, bias_c = column(gain[...]), column(bias[...])
    cell = lax.broadcasted_iota(jnp.int32, (1, CELLS), 1)
    row, col = cell >> 4, cell & 15
    for j in range(FRAMES + 2):
        clip, _, height, width = frame_facts(frames, res, jnp.maximum(first - 2 + j, 0))
        count = (frames[clip] * height * width * GS).astype(F32)
        mean = jnp.sum(jnp.where(lane == clip, totals, 0.0), axis=1, keepdims=True) / count
        square = jnp.sum(jnp.where(lane == clip + 4, totals, 0.0), axis=1, keepdims=True) / count
        rstd = lax.rsqrt(square - mean * mean + EPSILON)
        mean_c = jnp.concatenate([jnp.broadcast_to(mean[g : g + 1], (GS, 1)) for g in range(4)], axis=0)
        rstd_c = jnp.concatenate([jnp.broadcast_to(rstd[g : g + 1], (GS, 1)) for g in range(4)], axis=0)
        value = rim[j] if j < 2 else enc[j - 2]
        pre = (value.astype(F32) - mean_c) * rstd_c * gain_c + bias_c
        act = jnp.where(cell_valid(height, width), pre / (1.0 + jnp.exp(-pre)), 0.0)
        proj[j] = nn(taps[...], act.astype(BF16))
    results = []
    for f in range(FRAMES):
        _, start, _, _ = frame_facts(frames, res, first + f)
        source = [jnp.maximum(first + f - 2 + dt, start) - first + 2 for dt in range(3)]
        planes = [proj[source[dt], dt * 144 : (dt + 1) * 144, :] for dt in range(3)]
        joint = planes[0] + planes[1] + planes[2]
        result = jnp.zeros((LAT, CELLS), F32)
        for dx in range(3):
            part = jnp.zeros((LAT, CELLS), F32)
            for dy in range(3):
                tap = (dy * 3 + dx) * LAT
                piece = joint[tap : tap + LAT]
                if dy != 1:
                    piece = pltpu.roll(piece, (-(dy - 1) * SIDE) % CELLS, 1)
                    inside = (row >= 1) if dy == 0 else (row <= SIDE - 2)
                    piece = jnp.where(inside, piece, 0.0)
                part = part + piece
            if dx != 1:
                part = pltpu.roll(part, (-(dx - 1)) % CELLS, 1)
                inside = (col >= 1) if dx == 0 else (col <= SIDE - 2)
                part = jnp.where(inside, part, 0.0)
            result = result + part
        results.append(result.astype(BF16))
    sorted_cells = nn(jnp.concatenate(results, axis=0), cell_order()).astype(BF16)
    for ab in range(4):
        out[ab * LAT : (ab + 1) * LAT, :] = jnp.concatenate(
            [
                sorted_cells[f * LAT : (f + 1) * LAT, ab * 64 : (ab + 1) * 64]
                for f in range(FRAMES)
            ],
            axis=1,
        )


def shift_row(m_hi, m_lo, part):
    unit = jnp.where(lax.broadcasted_iota(jnp.int32, (16, AUG), 1) == FEAT + 1, 1.0, 0.0).astype(BF16)
    return (nt(unit, m_hi[part, :]) + nt(unit, m_lo[part, :]))[0:1]


def stacked(value):
    return jnp.concatenate([value[:, i : i + 128] for i in range(0, value.shape[1], 128)], axis=0)


def share_kernel(pair, one, two, three, out, total):
    value = (pair[...].astype(F32) + two[...].astype(F32)) + (one[...].astype(F32) + three[...].astype(F32))
    total[...] = value
    for j in range(out.shape[0]):
        out[j] = value.astype(BF16)


def cotangent_kernel(grad0, grad1, grad2, grad3, other0, other1, other2, other3, gate, w_out, lat_sorted, d_attn, d_out, latents):
    place = lax.axis_index("mp")
    core, level = lax.rem(place, 2), lax.div(place, 2)
    total = jnp.zeros((ROWS, HEADS * HD), F32)
    for k, grads in enumerate(((grad0, other0), (grad1, other1), (grad2, other2), (grad3, other3))):
        for side in range(2):
            m = lax.rem(level - k + 4, 4) * 2 + (core if side == 0 else 1 - core)
            cols = pl.ds(pl.multiple_of(m * 384, 128), 384)
            part = (grads[side][...].astype(F32) * gate[:, cols]).astype(BF16)
            d_attn[m] = part
            total = total + nt(part, w_out[:, cols])
    d_out[...] = total.astype(BF16)
    by_frame = jnp.concatenate(
        [
            jnp.concatenate(
                [lat_sorted[ab * LAT : (ab + 1) * LAT, f * 64 : (f + 1) * 64] for ab in range(4)], axis=1
            )
            for f in range(FRAMES)
        ],
        axis=0,
    )
    hi, lo = hi_lo(by_frame)
    order = cell_order()
    values = nt(hi, order) + nt(lo, order)
    for f in range(FRAMES):
        latents[f] = values[f * LAT : (f + 1) * LAT]


def prepare_kernel(
    embed_w,
    embed_b,
    shift,
    scale,
    w_hbm,
    gram_hi,
    gram_lo,
    m_hi,
    m_lo,
    m_k,
    centered_two,
    own_rows,
    window,
    w_qkv,
    arrived,
):
    fetch = pltpu.make_async_copy(w_hbm, w_qkv, arrived)
    fetch.start()
    row = lax.broadcasted_iota(jnp.int32, (16, D), 0)
    extra = jnp.where(row == 0, embed_b[...], 0.0)
    augmented = jnp.concatenate([nn(turn_back(), embed_w[...]), extra], axis=0)
    centered = augmented - jnp.mean(augmented, axis=1, keepdims=True)
    c_hi, c_lo = hi_lo(centered)
    centered_two[:AUG, :] = c_hi
    centered_two[AUG:, :] = c_lo
    gram = (nt(c_hi, c_hi) + nt(c_hi, c_lo) + nt(c_lo, c_hi)) * (1.0 / D)
    g_hi, g_lo = hi_lo(gram)
    gram_hi[...] = g_hi
    gram_lo[...] = g_lo
    row = lax.broadcasted_iota(jnp.int32, (AUG, D), 0)
    modulated = jnp.where(row == FEAT + 1, shift[...], centered * (1.0 + scale[...]))
    a_hi, a_lo = hi_lo(modulated)
    fetch.wait()
    both = nn(jnp.concatenate([a_hi, a_lo], axis=0), w_qkv[...])
    turned = (both[:AUG] + both[AUG:]).T
    t_hi, t_lo = hi_lo(turned)
    m_hi[...] = t_hi
    m_lo[...] = t_lo
    for h in range(HEADS):
        keys = slice(h * 384 + 128, h * 384 + 256)
        m_k[h * HD : (h + 1) * HD, :] = jnp.concatenate([t_hi[keys], t_hi[keys], t_lo[keys]], axis=1)
    window[...] = modulated.T
    slab = lax.axis_index("slab")
    o_hi, o_lo = hi_lo(window[pl.ds(pl.multiple_of(slab * 192, 64), 192), :])
    own_rows[...] = jnp.concatenate([o_hi, o_lo], axis=1)


def forward_kernel(
    frames,
    res,
    patches,
    place,
    gram_hi,
    gram_lo,
    m_k,
    m_hi,
    m_lo,
    d_out,
    q_gain,
    k_gain,
    grad_out,
    w_out,
    d_attn,
    embed_w,
    embed_b,
    gate,
    attn_mine,
    attn_other,
    g_part0,
    g_part1,
    g_part2,
    g_part3,
    hidden_cols,
    early,
    g_own,
    gate_cols,
    s_t,
    k_t,
    rk_t,
    q_ext,
    q_norm,
    q_facts,
    u_cat,
    s_own,
):
    blocks = patches.shape[0]
    row_aug = lax.broadcasted_iota(jnp.int32, (AUG, ROWS), 0)
    row16 = lax.broadcasted_iota(jnp.int32, (16, ROWS), 0)
    token = lax.broadcasted_iota(jnp.int32, (1, ROWS), 1)
    position = lax.broadcasted_iota(jnp.int32, (ROWS, ROWS), 0).astype(F32)
    base = (lax.axis_index("slab") * ROWS).astype(F32)
    k_gain_c = column(k_gain[...])
    one_row = jnp.where(row16 == 0, 1.0, 0.0).astype(BF16)

    def prepare(j, carry):
        x_q, clip_q = carry
        block = pl.ds(pl.multiple_of(j * ROWS, ROWS), ROWS)
        x_aug = jnp.concatenate([patches[j], one_row], axis=0)
        x_f = x_aug.astype(F32)
        gx = nn(gram_hi[...], x_aug) + nn(gram_lo[...], x_aug)
        rstd = lax.rsqrt(jnp.sum(gx * x_f, axis=0, keepdims=True) + EPSILON)
        s_hi, s_lo = hi_lo(jnp.where(row_aug == FEAT + 1, 1.0, x_f * rstd))
        s_t[:AUG, block] = s_hi
        s_t[AUG:, block] = s_lo
        clip = clip_number(frames, j * FRAMES + (token >> 6))
        height = jnp.zeros((1, ROWS), jnp.int32)
        width = jnp.zeros((1, ROWS), jnp.int32)
        for c in range(CLIPS):
            height = jnp.where(clip == c, res[c : c + 1, 0:1], height)
            width = jnp.where(clip == c, res[c : c + 1, 1:2], width)
        valid = (2 * ((token >> 3) & 7) < height) & (2 * (token & 7) < width)
        member = row16 == clip
        mask = jnp.where((row16 < CLIPS) & ~(member & valid), OFF, 0.0).astype(BF16)
        both = nn(m_k[...], jnp.concatenate([s_hi, s_lo, s_hi], axis=0))
        for h in range(HEADS):
            k = both[h * HD : (h + 1) * HD]
            rk = lax.rsqrt(jnp.mean(k * k, axis=0, keepdims=True) + EPSILON)
            rk_t[h, :, block] = jnp.broadcast_to(rk, (8, ROWS))
            k_t[h, :HD, block] = (k * rk * k_gain_c).astype(BF16)
            k_t[h, HD:, block] = mask
        spot = jnp.concatenate([place[j, 4:5, :], place[j, 5:6, :]], axis=1)
        chosen = jnp.where(spot == position + base, 1.0, 0.0).astype(BF16)
        x_q = x_q + nt(chosen, x_aug)
        clip_q = clip_q + nt(chosen, jnp.where(member, 1.0, 0.0).astype(BF16))
        return x_q, clip_q

    x_q, clip_q = lax.fori_loop(
        0, blocks, prepare, (jnp.zeros((ROWS, AUG), F32), jnp.zeros((ROWS, 16), F32)), unroll=PREPARE_UNROLL
    )
    x_qb = x_q.astype(BF16)
    own_cols = pl.ds(pl.multiple_of(lax.axis_index("mp") * 384, 128), 384)
    gate_cols[...] = gate[:, own_cols]
    embed_cols = nn(turn_back(), embed_w.ready()[:, own_cols]).astype(BF16)
    hidden_cols[...] = (nn(x_qb[:, :FEAT], embed_cols) + embed_b[:, own_cols]).astype(BF16)
    g_own[...] = stacked(nn(turn_rows(AUG), tn(x_qb, grad_out.ready()[...]).astype(BF16)))
    gx_q = nn(x_qb, gram_hi[...]) + nn(x_qb, gram_lo[...])
    rstd_q = lax.rsqrt(jnp.sum(gx_q * x_q, axis=1, keepdims=True) + EPSILON)
    lane_aug = lax.broadcasted_iota(jnp.int32, (ROWS, AUG), 1)
    s_q = jnp.where(lane_aug == FEAT + 1, 1.0, x_q * rstd_q)
    s_own[...] = s_q
    s_qhi, s_qlo = hi_lo(s_q)
    clip_qb = clip_q.astype(BF16)
    lane = lax.broadcasted_iota(jnp.int32, (ROWS, 128), 1)
    facts = jnp.zeros((ROWS, 128), F32)
    for h in range(HEADS):
        mine = slice(h * 384, h * 384 + 128)
        q = nt(s_qhi, m_hi[mine, :]) + nt(s_qlo, m_hi[mine, :]) + nt(s_qhi, m_lo[mine, :])
        rq = lax.rsqrt(jnp.mean(q * q, axis=1, keepdims=True) + EPSILON)
        qn = q * rq
        q_norm[h] = qn
        q_ext[h, :, :HD] = (qn * (q_gain[...] * (HD**-0.5 * LOG2E))).astype(BF16)
        q_ext[h, :, HD:] = clip_qb
        facts = jnp.where(lane == h, rq, facts)

    def forward(j, totals):
        block = pl.ds(pl.multiple_of(j * FWD_BLOCK, FWD_BLOCK), FWD_BLOCK)
        s_block = s_t[:, block]
        probs = [jnp.exp2(nn(q_ext[h], k_t[h, :, block])).astype(BF16) for h in range(HEADS)]
        return tuple(totals[h] + nt(probs[h], s_block) for h in range(HEADS))

    totals = lax.fori_loop(
        0, 4096 // FWD_BLOCK, forward, (jnp.zeros((ROWS, 2 * AUG), F32),) * HEADS, unroll=FWD_UNROLL
    )
    heads = []
    d_out = d_out.ready()
    for h in range(HEADS):
        inv_l = 1.0 / totals[h][:, FEAT + 1 : FEAT + 2]
        z_hi, z_lo = hi_lo((totals[h][:, :AUG] + totals[h][:, AUG:]) * inv_l)
        mine = slice(h * 384 + 256, h * 384 + 384)
        att = (nt(z_hi, m_hi[mine, :]) + nt(z_lo, m_hi[mine, :]) + nt(z_hi, m_lo[mine, :])).astype(BF16)
        heads.append(att)
        d_bf = d_out[:, h * HD : (h + 1) * HD]
        early[:, h * HD : (h + 1) * HD] = tn(z_hi, d_bf)
        do = d_bf.astype(F32)
        shift_v = shift_row(m_hi, m_lo, mine)
        weight = jnp.sum(do * (att.astype(F32) - shift_v), axis=1, keepdims=True) * inv_l
        facts = jnp.where(lane == 2 + h, weight, facts)
        u = (nn(d_bf, m_hi[mine, :]) + nn(d_bf, m_lo[mine, :])) * inv_l
        u_hi, u_lo = hi_lo(jnp.where(lane_aug == FEAT + 1, 0.0, u))
        u_cat[h] = jnp.concatenate([u_hi, u_lo, u_hi], axis=1)
    q_facts[...] = facts
    att_all = jnp.concatenate(heads, axis=1)
    place_mp, slab = lax.axis_index("mp"), lax.axis_index("slab")
    core = lax.rem(place_mp, 2)
    y_pos, x_pos = lax.div(slab, 4), lax.rem(slab, 4)
    d_attn, w_out = d_attn.ready(), w_out.ready()
    for k, g_part in enumerate((g_part0, g_part1, g_part2, g_part3)):
        y_to = lax.rem(y_pos + k, 4)
        for half in range(2):
            both = tn(d_attn[2 * y_to + half], att_all).astype(BF16)
            for side in range(2):
                slot = lax.rem(2 * half + side - x_pos + 4, 4)
                g_part.buffer[slot] = both[side * 192 : (side + 1) * 192]
        g_part.send()
    for side, attn_part in enumerate((attn_other, attn_mine)):
        for k in range(4):
            m = 2 * k + (core if side == 1 else 1 - core)
            cols = pl.ds(pl.multiple_of(m * 384, 128), 384)
            attn_part.buffer[k] = nn(att_all, w_out[:, cols]).astype(BF16)
        attn_part.send()


def backward_kernel(
    s_t,
    k_t,
    rk_t,
    q_ext,
    q_norm,
    q_facts,
    u_cat,
    s_own,
    m_hi,
    m_lo,
    q_gain,
    k_gain,
    early,
    mod_scale,
    centered,
    w_qkv,
    sums,
    y_mine,
    y_other,
    q_t,
):
    shift_k = []
    for h in range(HEADS):
        q_t[h] = q_ext[h, :, :HD].astype(F32).T.astype(BF16)
        mine = slice(h * 384 + 128, h * 384 + 256)
        shift_k.append(
            m_hi[mine, FEAT + 1 : FEAT + 2].astype(F32) + m_lo[mine, FEAT + 1 : FEAT + 2].astype(F32)
        )
    k_gain_c = column(k_gain[...])
    gain_back = k_gain_c * (1.0 / LOG2E)
    gain_inv = 1.0 / k_gain_c
    weights = [q_facts[:, 2 + h : 3 + h] for h in range(HEADS)]

    def backward(j, carry):
        grad_qs, p_k, quad = carry
        block = pl.ds(pl.multiple_of(j * BWD_BLOCK, BWD_BLOCK), BWD_BLOCK)
        s_hi = s_t[:AUG, block]
        s_cat = jnp.concatenate([s_hi, s_hi, s_t[AUG:, block]], axis=0)
        m2 = jnp.zeros((1, BWD_BLOCK), F32)
        new_q, dks = [], []
        for h in range(HEADS):
            keys = k_t[h, :HD, block]
            p = jnp.exp2(nn(q_ext[h], k_t[h, :, block]))
            raw = p * nn(u_cat[h], s_cat)
            m2 = m2 + jnp.sum(raw, axis=0, keepdims=True)
            d_score = (raw - p * weights[h]).astype(BF16)
            new_q.append(grad_qs[h] + nt(d_score, keys))
            scaled = nn(q_t[h], d_score) * gain_back
            kn = keys.astype(F32) * gain_inv
            rk = rk_t[h, 0:1, block]
            dk = rk * (scaled - kn * jnp.mean(scaled * kn, axis=0, keepdims=True))
            m2 = m2 + jnp.sum(dk * (kn * (1.0 / rk) - shift_k[h]), axis=0, keepdims=True)
            dks.append(dk.astype(BF16))
        p_k = p_k + nt(s_hi, jnp.concatenate(dks, axis=0))
        quad = quad + nt((s_hi.astype(F32) * m2).astype(BF16), s_hi)
        return tuple(new_q), p_k, quad

    grad_qs, p_k, quad = lax.fori_loop(
        0,
        4096 // BWD_BLOCK,
        backward,
        (
            (jnp.zeros((ROWS, HD), F32),) * HEADS,
            jnp.zeros((AUG, HEADS * HD), F32),
            jnp.zeros((AUG, AUG), F32),
        ),
        unroll=BWD_UNROLL,
    )
    s_q = s_own[...]
    s_qhi = s_q.astype(BF16)
    m2_q = jnp.zeros((ROWS, 1), F32)
    pieces = []
    for h in range(HEADS):
        mine = slice(h * 384, h * 384 + 128)
        rq = q_facts[:, h : h + 1]
        qn = q_norm[h]
        scaled = grad_qs[h] * (q_gain[...] * HD**-0.5)
        dq = rq * (scaled - qn * jnp.mean(scaled * qn, axis=1, keepdims=True))
        shift_q = shift_row(m_hi, m_lo, mine)
        m2_q = m2_q + jnp.sum(dq * (qn * (1.0 / rq) - shift_q), axis=1, keepdims=True)
        pieces += [tn(s_qhi, dq.astype(BF16)), p_k[:, h * HD : (h + 1) * HD], early[:, h * HD : (h + 1) * HD]]
    p_rows = jnp.concatenate(pieces, axis=1)
    p_all = p_rows.astype(BF16)
    extra = [p_rows[FEAT + i : FEAT + 1 + i, g * 128 : (g + 1) * 128] for i in range(2) for g in range(6)]
    extra = jnp.concatenate(extra + [jnp.zeros((4, 128), F32)], axis=0)
    sums[:384, :] = stacked(p_all[:FEAT])
    sums[384:, :] = extra.astype(BF16)
    quad = ((quad + tn((s_q * m2_q).astype(BF16), s_qhi)) * (1.0 / D)).astype(BF16)
    turn = turn_rows(AUG)
    turned = nn(turn, p_all).astype(BF16)
    quad = nn(turn, quad).astype(BF16)
    w_qkv = w_qkv.ready()
    back = nt(turned, w_qkv[...]) * (1.0 + mod_scale[...])
    back = back - jnp.mean(back, axis=1, keepdims=True)
    back = (back - nn(jnp.concatenate([quad, quad], axis=1), centered[...])).astype(BF16)
    place = lax.axis_index("mp")
    core, level = lax.rem(place, 2), lax.div(place, 2)
    for z in range(4):
        slot = lax.rem(z - level + 4, 4)
        even = back[:, 2 * z * 384 : (2 * z + 1) * 384]
        odd = back[:, (2 * z + 1) * 384 : (2 * z + 2) * 384]
        y_mine[slot] = stacked(jnp.where(core == 0, even, odd))
        y_other[slot] = stacked(jnp.where(core == 0, odd, even))


def attention_kernel(
    frames,
    res,
    patches,
    place,
    gram_hi,
    gram_lo,
    m_k,
    m_hi,
    m_lo,
    d_out,
    q_gain,
    k_gain,
    grad_out,
    w_out,
    d_attn,
    embed_w,
    embed_b,
    gate,
    mod_scale,
    centered,
    w_qkv,
    attn_mine,
    attn_other,
    g_part0,
    g_part1,
    g_part2,
    g_part3,
    hidden_cols,
    g_own,
    gate_cols,
    sums,
    y_mine,
    y_other,
    early,
    s_t,
    k_t,
    rk_t,
    q_ext,
    q_norm,
    q_facts,
    u_cat,
    s_own,
    q_t,
):
    forward_kernel(
        frames,
        res,
        patches,
        place,
        gram_hi,
        gram_lo,
        m_k,
        m_hi,
        m_lo,
        d_out,
        q_gain,
        k_gain,
        grad_out,
        w_out,
        d_attn,
        embed_w,
        embed_b,
        gate,
        attn_mine,
        attn_other,
        g_part0,
        g_part1,
        g_part2,
        g_part3,
        hidden_cols,
        early,
        g_own,
        gate_cols,
        s_t,
        k_t,
        rk_t,
        q_ext,
        q_norm,
        q_facts,
        u_cat,
        s_own,
    )
    backward_kernel(
        s_t,
        k_t,
        rk_t,
        q_ext,
        q_norm,
        q_facts,
        u_cat,
        s_own,
        m_hi,
        m_lo,
        q_gain,
        k_gain,
        early,
        mod_scale,
        centered.ready(),
        w_qkv,
        sums,
        y_mine,
        y_other,
        q_t,
    )


def weights_kernel(own, one, two, three, own_rows, g_qkv, g_embed):
    total = (own[...].astype(F32) + two[...].astype(F32)) + (one[...].astype(F32) + three[...].astype(F32))
    row = lax.broadcasted_iota(jnp.int32, (AUG, 128), 0)
    blocks = []
    for g in range(6):
        block = jnp.concatenate([total[g * 64 : (g + 1) * 64], jnp.zeros((AUG - FEAT, 128), F32)], axis=0)
        block = jnp.where(row == FEAT, total[384 + g : 385 + g], block)
        blocks.append(jnp.where(row == FEAT + 1, total[390 + g : 391 + g], block))
    p_all = jnp.concatenate(blocks, axis=1).astype(BF16)
    g_qkv[...] = nn(own_rows[...], jnp.concatenate([p_all, p_all], axis=0))
    for g in range(3):
        g_embed[:, g * 128 : (g + 1) * 128] = total[400 + g * 64 : 464 + g * 64]


VMEM = pl.BlockSpec(memory_space=pltpu.VMEM)
SMEM = pl.BlockSpec(memory_space=pltpu.SMEM)
ANY = pl.BlockSpec(memory_space=pl.ANY)


class Fetched:
    def __init__(self, source, buffer, sem):
        self.buffer, self.copy = buffer, pltpu.make_async_copy(source, buffer, sem)
        self.copy.start()

    def ready(self):
        self.copy.wait()
        return self.buffer


class Sent:
    def __init__(self, target, buffer, sem):
        self.buffer, self.copy = buffer, pltpu.make_async_copy(buffer, target, sem)

    def send(self):
        self.copy.start()


def call(kernel, inputs, outputs, scratch, flops, mib, places, out_places=None):
    single = not isinstance(outputs, tuple)
    outs = (outputs,) if single else outputs
    out_places = out_places or "v" * len(outs)
    staged = [
        (i, pltpu.VMEM(v.shape, v.dtype)) for i, (p, v) in enumerate(zip(places, inputs, strict=True)) if p == "l"
    ]
    sent = [(i, pltpu.VMEM(o.shape, o.dtype)) for i, (p, o) in enumerate(zip(out_places, outs, strict=True)) if p == "e"]
    n_in, n_out, n_stage, n_sent = len(inputs), len(outs), len(staged), len(sent)

    def wrapped(*refs):
        ins, results = list(refs[:n_in]), list(refs[n_in : n_in + n_out])
        rest = refs[n_in + n_out :]
        buffers, rest = rest[:n_stage], rest[n_stage:]
        holds, rest = rest[:n_sent], rest[n_sent:]
        sems, rest = rest[: n_stage + n_sent], rest[n_stage + n_sent :]
        for slot, (i, _) in enumerate(staged):
            ins[i] = Fetched(ins[i], buffers[slot], sems[slot])
        for slot, (i, _) in enumerate(sent):
            results[i] = Sent(results[i], holds[slot], sems[n_stage + slot])
        kernel(*ins, *results, *rest)
        for i, _ in sent:
            results[i].copy.wait()

    specs = {"v": VMEM, "e": ANY, "l": ANY, "r": ANY, "s": SMEM}
    result = pl.pallas_call(
        wrapped,
        out_shape=outs,
        in_specs=[specs[p] for p in places],
        out_specs=tuple(specs[p] for p in out_places),
        scratch_shapes=[b for _, b in staged]
        + [b for _, b in sent]
        + [pltpu.SemaphoreType.DMA] * (n_stage + n_sent)
        + scratch,
        compiler_params=pltpu.CompilerParams(vmem_limit_bytes=mib * MIB),
        cost_estimate=pl.CostEstimate(flops=flops, bytes_accessed=1 << 20, transcendentals=0),
    )(*inputs)
    return result[0] if single else result


def shift_by(value, axis, move):
    return lax.ppermute(value, axis, [(i, move(i)) for i in range(lax.axis_size(axis))])


def along_x(k):
    return lambda i: (i // 4) * 4 + (i % 4 + k) % 4


def along_y(k):
    return lambda i: ((i // 4 + k) % 4) * 4 + i % 4


def along_z(k):
    return lambda i: ((i // 2 + k) % 4) * 2 + i % 2


def sum_of_four(value, axis, move, kind):
    sent = value.astype(kind)
    one, two, three = (shift_by(sent, axis, move(k)).astype(F32) for k in (1, 2, 3))
    return (sent.astype(F32) + two) + (one + three)


Z_GROUPS = [[0, 2, 4, 6], [1, 3, 5, 7]]


def level_sum(pair):
    one, two, three = (shift_by(pair[k], "mp", along_z(k)).astype(F32) for k in (1, 2, 3))
    return (pair[0].astype(F32) + two) + (one + three)


def body(
    enc_feat,
    gn_gain,
    gn_bias,
    conv_w,
    clip_frames,
    clip_res,
    token_place,
    embed_w,
    embed_b,
    mod_shift,
    mod_scale,
    mod_gate,
    w_qkv,
    q_gain,
    k_gain,
    w_out,
    grad_out,
):
    slabs = lax.axis_size("slab")
    mp_size = lax.axis_size("mp")
    cols_dev = D // mp_size
    row_cols = D // slabs

    clip_res = jnp.pad(clip_res, ((0, 4), (0, 126)))
    all_sent = call(
        stats_kernel,
        (clip_frames, clip_res, enc_feat, token_place.reshape(2, 128)),
        jax.ShapeDtypeStruct((slabs, 8, 128), F32),
        [],
        1 << 20,
        60,
        "svvv",
    )
    all_stats = lax.all_to_all(all_sent, "slab", split_axis=0, concat_axis=0, tiled=True)
    rim = shift_by(enc_feat[FRAMES - 2 :], "slab", lambda i: (i + 1) % slabs)
    rim, grad_sent = lax.optimization_barrier((rim, grad_out))
    grads = (grad_sent,) + tuple(shift_by(grad_sent, "mp", along_z(k)) for k in (1, 2, 3))
    taps = call(
        taps_kernel,
        (conv_w,),
        jax.ShapeDtypeStruct((432, FEAT), BF16),
        [],
        1 << 33,
        60,
        "v",
    )
    partial = call(
        conv_kernel,
        (clip_frames, clip_res, enc_feat, rim, all_stats, gn_gain[None, :], gn_bias[None, :], taps),
        jax.ShapeDtypeStruct((FEAT, CELLS), BF16),
        [pltpu.VMEM((FRAMES + 2, 432, CELLS), F32)],
        1 << 28,
        60,
        "svvvvvvv",
    )
    partial, grads = lax.optimization_barrier((partial, grads))
    pair = (partial.astype(F32) + shift_by(partial, "mp", lambda i: i ^ 1).astype(F32)).astype(BF16)
    patches_sent, lat_sorted = call(
        share_kernel,
        (pair,) + tuple(shift_by(pair, "mp", along_z(k)) for k in (1, 2, 3)),
        (
            jax.ShapeDtypeStruct((slabs, FEAT, CELLS), BF16),
            jax.ShapeDtypeStruct((FEAT, CELLS), F32),
        ),
        [],
        1 << 20,
        4,
        "vvvv",
    )
    all_patches = lax.all_to_all(patches_sent, "slab", split_axis=0, concat_axis=0, tiled=True)

    embed_late, _ = lax.optimization_barrier((embed_b, patches_sent))
    gram_hi, gram_lo, m_hi, m_lo, m_k, centered, own_rows = call(
        prepare_kernel,
        (embed_w, embed_late[None, :], mod_shift[None, :], mod_scale[None, :], w_qkv),
        (
            jax.ShapeDtypeStruct((AUG, AUG), BF16),
            jax.ShapeDtypeStruct((AUG, AUG), BF16),
            jax.ShapeDtypeStruct((768, AUG), BF16),
            jax.ShapeDtypeStruct((768, AUG), BF16),
            jax.ShapeDtypeStruct((HEADS * HD, 3 * AUG), BF16),
            jax.ShapeDtypeStruct((2 * AUG, D), BF16),
            jax.ShapeDtypeStruct((row_cols, 2 * AUG), BF16),
        ),
        [pltpu.VMEM((D, AUG), F32), pltpu.VMEM((D, 768), BF16), pltpu.SemaphoreType.DMA],
        1 << 32,
        60,
        "vvvvr",
    )

    grads, lat_sorted = lax.optimization_barrier((grads, lat_sorted))
    others = tuple(shift_by(block, "mp", lambda i: i ^ 1) for block in grads)
    d_attn, d_out, latents = call(
        cotangent_kernel,
        (*grads, *others, mod_gate[None, :], w_out, lat_sorted),
        (
            jax.ShapeDtypeStruct((mp_size, ROWS, cols_dev), BF16),
            jax.ShapeDtypeStruct((ROWS, HEADS * HD), BF16),
            jax.ShapeDtypeStruct((FRAMES, LAT, CELLS), F32),
        ),
        [],
        1 << 32,
        60,
        "vvvvvvvvvvv",
    )

    attn_mine, attn_other, *g_parts, hidden_cols, g_own, gate_cols, sums, y_mine, y_other = call(
        attention_kernel,
        (
            clip_frames,
            clip_res,
            all_patches,
            all_stats,
            gram_hi,
            gram_lo,
            m_k,
            m_hi,
            m_lo,
            d_out,
            q_gain[None, :],
            k_gain[None, :],
            grad_out,
            w_out,
            d_attn,
            embed_w,
            embed_b[None, :],
            mod_gate[None, :],
            mod_scale[None, :],
            centered,
            w_qkv,
        ),
        (
            *(jax.ShapeDtypeStruct((4, ROWS, cols_dev), BF16),) * 2,
            *(jax.ShapeDtypeStruct((4, row_cols, HEADS * HD), BF16),) * 4,
            jax.ShapeDtypeStruct((ROWS, cols_dev), BF16),
            jax.ShapeDtypeStruct((192, 128), F32),
            jax.ShapeDtypeStruct((1, cols_dev), F32),
            jax.ShapeDtypeStruct((400, 128), BF16),
            jax.ShapeDtypeStruct((4, 192, 128), BF16),
            jax.ShapeDtypeStruct((4, 192, 128), BF16),
        ),
        [
            pltpu.VMEM((AUG, 256), F32),
            pltpu.VMEM((2 * AUG, 4096), BF16),
            pltpu.VMEM((HEADS, EXT, 4096), BF16),
            pltpu.VMEM((HEADS, 8, 4096), F32),
            pltpu.VMEM((HEADS, ROWS, EXT), BF16),
            pltpu.VMEM((HEADS, ROWS, HD), F32),
            pltpu.VMEM((ROWS, 128), F32),
            pltpu.VMEM((HEADS, ROWS, 3 * AUG), BF16),
            pltpu.VMEM((ROWS, AUG), F32),
            pltpu.VMEM((HEADS, HD, ROWS), BF16),
        ],
        1 << 34,
        60,
        "svvvvvvvvlvvllllvvvll",
        "eeeeeevvvvvv",
    )

    y_got = shift_by(y_other, "mp", lambda i: i ^ 1)
    y_pair = (y_mine.astype(F32) + y_got.astype(F32)).astype(BF16)
    y_pair, attn_other, g_parts = lax.optimization_barrier((y_pair, attn_other, g_parts))
    attn_got = shift_by(attn_other, "mp", lambda i: i ^ 1)
    g_one, g_two, g_three = (shift_by(g_parts[k], "slab", along_y(k)) for k in (1, 2, 3))
    embed_part = level_sum(y_pair) + g_own
    payload = jnp.concatenate([sums, embed_part.astype(BF16)], axis=0)
    payload, attn_mine = lax.optimization_barrier((payload, attn_mine))
    payload, g_one = lax.optimization_barrier((payload, g_one))
    sent = tuple(shift_by(payload, "slab", along_x(k)) for k in (1, 2, 3))
    sent, g_two, g_three = lax.optimization_barrier((sent, g_two, g_three))
    total = (
        (payload.astype(F32) + sent[1].astype(F32)) + (sent[0].astype(F32) + sent[2].astype(F32))
    ).astype(BF16)
    attn_pair = (attn_mine.astype(F32) + attn_got.astype(F32)).astype(BF16)
    attn_got = lax.all_to_all(attn_pair, "mp", split_axis=0, concat_axis=0, tiled=True, axis_index_groups=Z_GROUPS)
    total, attn_got = lax.optimization_barrier((total, attn_got))
    received = tuple(shift_by(total, "slab", along_y(k)) for k in (1, 2, 3))
    total, g_two = lax.optimization_barrier((total, g_two))
    g_sum = (
        (g_parts[0].astype(F32) + g_two.astype(F32)) + (g_one.astype(F32) + g_three.astype(F32))
    ).astype(BF16)
    g_got = tuple(shift_by(g_sum[k], "slab", along_x(k)) for k in (1, 2, 3))
    received, g_late = lax.optimization_barrier((received, g_sum[0]))
    attn_cols = jnp.sum(attn_got.astype(F32), axis=0)
    block_out = (hidden_cols.astype(F32) + gate_cols * attn_cols).astype(BF16)
    g_out = (
        (g_late.astype(F32) + g_got[1].astype(F32)) + (g_got[0].astype(F32) + g_got[2].astype(F32))
    ).T
    g_qkv, g_embed = call(
        weights_kernel,
        (total, *received, own_rows),
        (
            jax.ShapeDtypeStruct((row_cols, 768), F32),
            jax.ShapeDtypeStruct((FEAT, cols_dev), F32),
        ),
        [],
        1 << 26,
        4,
        "vvvvv",
    )
    return (latents, block_out, g_qkv, g_out, g_embed)


def solution(mesh):
    in_specs = (
        P(("dp", "slab"), "mp", None),
        P("mp"),
        P("mp"),
        P("mp", None),
        P("dp"),
        P("dp", None),
        P(("dp", "slab")),
        P(),
        P(),
        P("dp"),
        P("dp"),
        P("dp"),
        P(None, "mp"),
        P(),
        P(),
        P("mp", None),
        P(("dp", "slab"), "mp"),
    )
    out_specs = (
        P(("dp", "slab"), None, None),
        P(("dp", "slab"), "mp"),
        P(("dp", "slab"), "mp"),
        P(("dp", "mp"), "slab"),
        P("dp", "mp"),
    )
    return jax.shard_map(body, mesh=mesh, in_specs=in_specs, out_specs=out_specs, check_vma=False)
```
